32 devices in a mesh: batch: 2 (over x), ulysses: 4 (over y, core), shard: 4 (over z).
Axes of the slice: x: 2, y: 2, z: 4, core: 2. Of those that a mesh axis runs over, the one named last changes fastest.
Arguments:
- hidden: bfloat16 [4096, 1024], P(('batch', 'ulysses', 'shard')), may hold values from -6 to 6
- ln1_gain: bfloat16 [1024], P(('batch', 'ulysses', 'shard')), may hold values from 0.5 to 1.5
- ln1_bias: bfloat16 [1024], P(('batch', 'ulysses', 'shard')), may hold values from -1.5 to 1.5
- qkv_weight: bfloat16 [1024, 3072], P(('batch', 'ulysses', 'shard')), may hold values from -0.1875 to 0.1875
- qv_bias: bfloat16 [2048], P(('batch', 'ulysses', 'shard')), may hold values from -2.5 to 2.5
- out_weight: bfloat16 [1024, 1024], P(('batch', 'ulysses', 'shard')), may hold values from -0.75 to 0.75
- out_bias: bfloat16 [1024], P(('batch', 'ulysses', 'shard')), may hold values from -1.5 to 1.5
- ln2_gain: bfloat16 [1024], P(('batch', 'ulysses', 'shard')), may hold values from 0.5 to 1.5
- ln2_bias: bfloat16 [1024], P(('batch', 'ulysses', 'shard')), may hold values from -1.5 to 1.5
- fc1_weight: bfloat16 [1024, 4096], P(('batch', 'ulysses', 'shard')), may hold values from -0.1875 to 0.1875
- fc1_bias: bfloat16 [4096], P(('batch', 'ulysses', 'shard')), may hold values from -2.5 to 2.5
- fc2_weight: bfloat16 [4096, 1024], P(('batch', 'ulysses', 'shard')), may hold values from -0.09375 to 0.09375
- fc2_bias: bfloat16 [1024], P(('batch', 'ulysses', 'shard')), may hold values from -1.5 to 1.5
- cotangent: bfloat16 [4096, 1024], P(('batch', 'ulysses', 'shard')), may hold values from -6 to 6
Outputs:
- output: float32 [4096, 1024], P(('batch', 'ulysses', 'shard'))
- input_grad: float32 [4096, 1024], P(('batch', 'ulysses', 'shard'))
- ln1_gain_grad: float32 [1024], P(('batch', 'ulysses', 'shard'))
- ln1_bias_grad: float32 [1024], P(('batch', 'ulysses', 'shard'))
- qkv_weight_grad: float32 [1024, 3072], P(('batch', 'ulysses', 'shard'))
- qv_bias_grad: float32 [2048], P(('batch', 'ulysses', 'shard'))
- out_weight_grad: float32 [1024, 1024], P(('batch', 'ulysses', 'shard'))
- out_bias_grad: float32 [1024], P(('batch', 'ulysses', 'shard'))
- ln2_gain_grad: float32 [1024], P(('batch', 'ulysses', 'shard'))
- ln2_bias_grad: float32 [1024], P(('batch', 'ulysses', 'shard'))
- fc1_weight_grad: float32 [1024, 4096], P(('batch', 'ulysses', 'shard'))
- fc1_bias_grad: float32 [4096], P(('batch', 'ulysses', 'shard'))
- fc2_weight_grad: float32 [4096, 1024], P(('batch', 'ulysses', 'shard'))
- fc2_bias_grad: float32 [1024], P(('batch', 'ulysses', 'shard'))
The draws below stay inside these ranges and needn't reach their ends.
All inputs are finite; a program needn't handle non-finite values.
Results may differ from the reference program's by a relative error of at most 0.01.
Values may be sent and summed in bfloat16 or wider, within the bound.
No kernel may reach another device: no remote copies, remote signals or barrier semaphores. Data moves between devices by JAX's collectives and lax.ppermute only.
A program may use at most 192 MiB of HBM per device.

```python
import math
import jax
import jax.numpy as jnp
from jax import lax

D = 1024
HEADS = 16
HD = 64
FF = 4096
KT = 256
SEQ = 2048
SEQS = 2
TOKENS = 4096


def level_of(own_key, dims, pieces, low, high):
    def one(position, shards_of):
        heights = jax.random.uniform(jax.random.fold_in(jax.random.fold_in(own_key, 6), position), (shards_of,), jnp.float32, low / len(pieces), high / len(pieces))
        return jnp.repeat(jnp.exp(heights), dims[position] // shards_of).reshape((-1,) + (1,) * (len(dims) - position - 1))

    level = one(*pieces[0])
    for cut in pieces[1:]:
        level = level * one(*cut)
    return level


def normal_values(stream_key, shape, deviation, reach, shards=(), held_as=jnp.bfloat16):
    factor_of = level_of(stream_key, shape, shards, -0.22, 0.18) if shards else 1.0
    entries = jax.random.normal(stream_key, shape, jnp.float32) * deviation * factor_of
    return jnp.minimum(jnp.maximum(entries, -reach), reach).astype(held_as)


def setup_inputs(seed: int = 0) -> dict:
    key_list = jax.random.split(jax.random.key(seed), 15)
    return {
        "hidden": normal_values(key_list[0], (TOKENS, D), 1.0, 6.0, ((0, 32),)),
        "ln1_gain": jnp.clip(1.0 + 0.1 * jax.random.normal(key_list[1], (D,), jnp.float32), 0.5, 1.5).astype(jnp.bfloat16),
        "ln1_bias": normal_values(key_list[2], (D,), 0.3, 1.5, ((0, 32),)),
        "qkv_weight": normal_values(key_list[3], (D, 3 * D), D ** -0.5, 0.1875, ((0, 32),)),
        "qv_bias": normal_values(key_list[4], (2 * D,), 0.5, 2.5, ((0, 32),)),
        "out_weight": normal_values(key_list[5], (D, D), (D // 16) ** -0.5, 0.75, ((0, 32),)),
        "out_bias": normal_values(key_list[6], (D,), 0.3, 1.5, ((0, 32),)),
        "ln2_gain": jnp.clip(1.0 + 0.1 * jax.random.normal(key_list[7], (D,), jnp.float32), 0.5, 1.5).astype(jnp.bfloat16),
        "ln2_bias": normal_values(key_list[8], (D,), 0.3, 1.5, ((0, 32),)),
        "fc1_weight": normal_values(key_list[9], (D, FF), D ** -0.5, 0.1875, ((0, 32),)),
        "fc1_bias": normal_values(key_list[10], (FF,), 0.5, 2.5, ((0, 32),)),
        "fc2_weight": normal_values(key_list[11], (FF, D), FF ** -0.5, 0.09375, ((0, 32),)),
        "fc2_bias": normal_values(key_list[12], (D,), 0.3, 1.5, ((0, 32),)),
        "cotangent": normal_values(key_list[13], (TOKENS, D), 1.0, 6.0, ((0, 32),)),
    }


norm_eps = 1e-05
gelu_coef = 0.7978845608028654

def normalize(inputs, gain, shift):
    center = lax.optimization_barrier(jnp.mean(inputs, axis=-1, keepdims=True))
    centred = inputs - center
    variance = lax.optimization_barrier(jnp.mean(centred * centred, axis=-1, keepdims=True))
    inverse = lax.rsqrt(variance + norm_eps)
    unit_rows = centred * inverse
    return (unit_rows * gain + shift, unit_rows, inverse)

def normalize_back(grad_out, unit_rows, inverse, gain):
    grad_unit = grad_out * gain
    first = lax.optimization_barrier(jnp.mean(grad_unit, axis=-1, keepdims=True))
    second = lax.optimization_barrier(jnp.mean(grad_unit * unit_rows, axis=-1, keepdims=True))
    grad_in = inverse * (grad_unit - first - unit_rows * second)
    return (grad_in, lax.optimization_barrier(jnp.sum(grad_out * unit_rows, axis=0)), lax.optimization_barrier(jnp.sum(grad_out, axis=0)))

def gelu_value(pre_act):
    inner = gelu_coef * (pre_act + 0.044715 * pre_act * pre_act * pre_act)
    return 0.5 * pre_act * (1.0 + jnp.tanh(inner))

def gelu_slope(pre_act):
    inner = gelu_coef * (pre_act + 0.044715 * pre_act * pre_act * pre_act)
    tanh_val = jnp.tanh(inner)
    return 0.5 * (1.0 + tanh_val) + 0.5 * pre_act * (1.0 - tanh_val * tanh_val) * gelu_coef * (1.0 + 3.0 * 0.044715 * pre_act * pre_act)

def joined_shift(qv_shift):
    pairs = qv_shift.astype(jnp.float32).reshape(HEADS, 2, HD)
    return jnp.stack([pairs[:, 0], jnp.zeros_like(pairs[:, 0]), pairs[:, 1]], axis=1).reshape(3 * D)

def forward_head(operands):
    queries, keys, values, slope = operands
    length = queries.shape[0]
    rows = min(512, length)
    factor_scale = 1.0 / math.sqrt(HD)
    key_tiles = keys.reshape(length // KT, KT, HD)
    value_tiles = values.reshape(length // KT, KT, HD)
    tile_starts = jnp.arange(length // KT, dtype=jnp.int32) * KT

    def one_block(start):
        block = lax.dynamic_slice_in_dim(queries, start, rows, 0)
        query_pos = start + jnp.arange(rows, dtype=jnp.int32)

        def one_tile(state, tile):
            top, total, accum = state
            key_tile, value_tile, tile_start = tile
            key_pos = tile_start + jnp.arange(KT, dtype=jnp.int32)
            scores = jnp.dot(block, key_tile.T, preferred_element_type=jnp.float32) * factor_scale
            scores = scores - slope * (query_pos[:, None] - key_pos[None, :]).astype(jnp.float32)
            scores = jnp.where(key_pos[None, :] <= query_pos[:, None], scores, -jnp.inf)
            new_top = jnp.maximum(top, lax.optimization_barrier(jnp.max(scores, axis=1)))
            weights = jnp.exp(scores - new_top[:, None])
            decay = jnp.exp(top - new_top)
            total = total * decay + lax.optimization_barrier(jnp.sum(weights, axis=1))
            accum = accum * decay[:, None] + jnp.dot(weights.astype(jnp.bfloat16), value_tile, preferred_element_type=jnp.float32)
            return ((new_top, total, accum), None)
        start_state = (jnp.full((rows,), -jnp.inf, jnp.float32), jnp.zeros((rows,), jnp.float32), jnp.zeros((rows, HD), jnp.float32))
        (top, total, accum), unused = lax.scan(one_tile, start_state, (key_tiles, value_tiles, tile_starts))
        return ((accum / total[:, None]).astype(jnp.bfloat16), top + jnp.log(total))
    outs, lse = lax.map(one_block, jnp.arange(length // rows, dtype=jnp.int32) * rows)
    return (outs.reshape(length, HD), lse.reshape(length))

def backward_head(operands):
    queries, keys, values, outs, grad_outs, lse, slope = operands
    length = queries.shape[0]
    rows = min(512, length)
    factor_scale = 1.0 / math.sqrt(HD)
    delta = lax.optimization_barrier(jnp.sum(grad_outs.astype(jnp.float32) * outs.astype(jnp.float32), axis=1))
    key_pos = jnp.arange(length, dtype=jnp.int32)

    def one_block(state, start):
        grad_keys, grad_values = state
        block = lax.dynamic_slice_in_dim(queries, start, rows, 0)
        grad_block = lax.dynamic_slice_in_dim(grad_outs, start, rows, 0)
        lse_block = lax.dynamic_slice_in_dim(lse, start, rows, 0)
        delta_block = lax.dynamic_slice_in_dim(delta, start, rows, 0)
        query_pos = start + jnp.arange(rows, dtype=jnp.int32)
        scores = jnp.dot(block, keys.T, preferred_element_type=jnp.float32) * factor_scale
        scores = scores - slope * (query_pos[:, None] - key_pos[None, :]).astype(jnp.float32)
        probs = jnp.where(key_pos[None, :] <= query_pos[:, None], jnp.exp(scores - lse_block[:, None]), 0.0)
        grad_values = grad_values + jnp.dot(probs.astype(jnp.bfloat16).T, grad_block, preferred_element_type=jnp.float32)
        grad_probs = jnp.dot(grad_block, values.T, preferred_element_type=jnp.float32)
        grad_scores = (probs * (grad_probs - delta_block[:, None]) * factor_scale).astype(jnp.bfloat16)
        grad_query = jnp.dot(grad_scores, keys, preferred_element_type=jnp.float32)
        grad_keys = grad_keys + jnp.dot(grad_scores.T, block, preferred_element_type=jnp.float32)
        return ((grad_keys, grad_values), grad_query)
    zero_rows = jnp.zeros((length, HD), jnp.float32)
    (grad_keys, grad_values), grad_query = lax.scan(one_block, (zero_rows, zero_rows), jnp.arange(length // rows, dtype=jnp.int32) * rows)
    return (grad_query.reshape(length, HD), grad_keys, grad_values)

def one_sequence(params, seq_in, seq_grad):
    gain_one, shift_one, w_qkv, qv_shift, w_out, out_shift, gain_two, shift_two, w_up, up_shift, w_down, down_shift = params
    length = seq_in.shape[0]
    slopes = jnp.exp2(-8.0 * (jnp.arange(HEADS, dtype=jnp.float32) + 1.0) / HEADS)
    inputs = seq_in.astype(jnp.float32)
    normed_one, unit_one, inv_one = normalize(inputs, gain_one.astype(jnp.float32), shift_one.astype(jnp.float32))
    normed_one = normed_one.astype(jnp.bfloat16)
    joined = (jnp.dot(normed_one, w_qkv, preferred_element_type=jnp.float32) + joined_shift(qv_shift)).astype(jnp.bfloat16)
    parts = joined.reshape(length, HEADS, 3, HD).transpose(1, 2, 0, 3)
    queries, keys, values = (parts[:, 0], parts[:, 1], parts[:, 2])
    context, lse = lax.map(forward_head, (queries, keys, values, slopes))
    context_rows = context.transpose(1, 0, 2).reshape(length, D)
    attended = inputs + (jnp.dot(context_rows, w_out, preferred_element_type=jnp.float32) + out_shift.astype(jnp.float32))
    normed_two, unit_two, inv_two = normalize(attended, gain_two.astype(jnp.float32), shift_two.astype(jnp.float32))
    normed_two = normed_two.astype(jnp.bfloat16)
    pre_act = jnp.dot(normed_two, w_up, preferred_element_type=jnp.float32) + up_shift.astype(jnp.float32)
    activated = gelu_value(pre_act).astype(jnp.bfloat16)
    output = jnp.dot(activated, w_down, preferred_element_type=jnp.float32) + down_shift.astype(jnp.float32) + attended
    grad_float = seq_grad.astype(jnp.float32)
    grad_down_w = jnp.dot(activated.T, seq_grad, preferred_element_type=jnp.float32)
    grad_down_b = lax.optimization_barrier(jnp.sum(grad_float, axis=0))
    grad_pre = (jnp.dot(seq_grad, w_down.T, preferred_element_type=jnp.float32) * gelu_slope(pre_act)).astype(jnp.bfloat16)
    grad_up_w = jnp.dot(normed_two.T, grad_pre, preferred_element_type=jnp.float32)
    grad_up_b = lax.optimization_barrier(jnp.sum(grad_pre.astype(jnp.float32), axis=0))
    grad_norm_two = jnp.dot(grad_pre, w_up.T, preferred_element_type=jnp.float32)
    grad_in_two, grad_gain_two, grad_shift_two = normalize_back(grad_norm_two, unit_two, inv_two, gain_two.astype(jnp.float32))
    grad_attended = grad_float + grad_in_two
    grad_round = grad_attended.astype(jnp.bfloat16)
    grad_out_w = jnp.dot(context_rows.T, grad_round, preferred_element_type=jnp.float32)
    grad_out_b = lax.optimization_barrier(jnp.sum(grad_attended, axis=0))
    grad_context = jnp.dot(grad_round, w_out.T, preferred_element_type=jnp.float32).astype(jnp.bfloat16)
    grad_heads = grad_context.reshape(length, HEADS, HD).transpose(1, 0, 2)
    grad_query, grad_keys, grad_values = lax.map(backward_head, (queries, keys, values, context, grad_heads, lse, slopes))
    grad_qkv = jnp.stack([grad_query, grad_keys, grad_values], axis=1).transpose(2, 0, 1, 3).reshape(length, 3 * D).astype(jnp.bfloat16)
    grad_qkv_w = jnp.dot(normed_one.T, grad_qkv, preferred_element_type=jnp.float32)
    column_sums = lax.optimization_barrier(jnp.sum(grad_qkv.astype(jnp.float32), axis=0)).reshape(HEADS, 3, HD)
    grad_qv = jnp.stack([column_sums[:, 0], column_sums[:, 2]], axis=1).reshape(2 * D)
    grad_norm_one = jnp.dot(grad_qkv, w_qkv.T, preferred_element_type=jnp.float32)
    grad_in_one, grad_gain_one, grad_shift_one = normalize_back(grad_norm_one, unit_one, inv_one, gain_one.astype(jnp.float32))
    input_grad = grad_attended + grad_in_one
    grads = (grad_gain_one, grad_shift_one, grad_qkv_w, grad_qv, grad_out_w, grad_out_b, grad_gain_two, grad_shift_two, grad_up_w, grad_up_b, grad_down_w, grad_down_b)
    return (output, input_grad, grads)

def reference(hidden, ln1_gain, ln1_bias, qkv_weight, qv_bias, out_weight, out_bias, ln2_gain, ln2_bias, fc1_weight, fc1_bias, fc2_weight, fc2_bias, cotangent):
    params = (ln1_gain, ln1_bias, qkv_weight, qv_bias, out_weight, out_bias, ln2_gain, ln2_bias, fc1_weight, fc1_bias, fc2_weight, fc2_bias)

    def step(totals, operands):
        seq_in, seq_grad = operands
        output, input_grad, grads = one_sequence(params, seq_in, seq_grad)
        return (jax.tree.map(lambda left, right: left + right, totals, grads), (output, input_grad))
    zero_grads = tuple((jnp.zeros(param.shape, jnp.float32) for param in params))
    totals, (outputs, input_grads) = lax.scan(step, zero_grads, (hidden.reshape(SEQS, SEQ, D), cotangent.reshape(SEQS, SEQ, D)))
    return (outputs.reshape(TOKENS, D), input_grads.reshape(TOKENS, D), totals[0], totals[1], totals[2], totals[3], totals[4], totals[5], totals[6], totals[7], totals[8], totals[9], totals[10], totals[11])
```

```python
import functools
import math

import jax
import jax.numpy as jnp
from jax import lax
from jax.experimental import pallas as pl
from jax.experimental.pallas import tpu as pltpu
from jax.sharding import PartitionSpec as P

D = 1024
HEADS = 16
HD = 64

norm_eps = 1e-05
gelu_coef = 0.7978845608028654

ALL = ("batch", "ulysses", "shard")
SEQUENCE = ("ulysses", "shard")
PLANE = ("batch", "ulysses")
bf16 = jnp.bfloat16
f32 = jnp.float32


def normalize(inputs, gain, shift):
    center = jnp.mean(inputs, axis=-1, keepdims=True)
    centred = inputs - center
    variance = jnp.mean(centred * centred, axis=-1, keepdims=True)
    inverse = lax.rsqrt(variance + norm_eps)
    unit_rows = centred * inverse
    return (unit_rows * gain + shift, unit_rows, inverse)


def normalize_back(grad_out, unit_rows, inverse, gain):
    grad_unit = grad_out * gain
    first = jnp.mean(grad_unit, axis=-1, keepdims=True)
    second = jnp.mean(grad_unit * unit_rows, axis=-1, keepdims=True)
    grad_in = inverse * (grad_unit - first - unit_rows * second)
    return (grad_in, jnp.sum(grad_out * unit_rows, axis=0), jnp.sum(grad_out, axis=0))


def gelu_both(pre_act):
    inner = gelu_coef * (pre_act + 0.044715 * pre_act * pre_act * pre_act)
    tanh_val = jnp.tanh(inner)
    value = 0.5 * pre_act * (1.0 + tanh_val)
    slope = 0.5 * (1.0 + tanh_val) + 0.5 * pre_act * (1.0 - tanh_val * tanh_val) * gelu_coef * (
        1.0 + 3.0 * 0.044715 * pre_act * pre_act
    )
    return (value, slope)


def three_parts(column):
    high = column.astype(bf16)
    rest = column - high.astype(f32)
    middle = rest.astype(bf16)
    low = (rest - middle.astype(f32)).astype(bf16)
    return (high, middle, low)


def dot_last(left, right):
    return lax.dot_general(left, right, (((1,), (1,)), ((), ())), preferred_element_type=f32)


def forward_kernel(block, qkv_ref, slope_ref, context_ref, q_ref, k_ref, v_ref):
    length = qkv_ref.shape[0]
    slope = slope_ref[0]
    for start in range(0, length, block):
        rows = pl.ds(start, block)
        qkv = qkv_ref[rows, :]
        zeros = jnp.zeros((block, HD - 6), bf16)
        ones = jnp.ones((block, 3), bf16)
        position = start + lax.broadcasted_iota(jnp.int32, (block, 1), 0)
        bias = three_parts(position.astype(f32) * slope)
        k_ref[rows, :] = jnp.concatenate([qkv[:, HD : 2 * HD], *bias, ones, zeros], axis=1)
        v_ref[rows, :] = jnp.concatenate(
            [qkv[:, 2 * HD : 3 * HD], ones, jnp.zeros((block, HD - 3), bf16)], axis=1
        )
    key_id = lax.broadcasted_iota(jnp.int32, (block, block), 1)
    row_id = lax.broadcasted_iota(jnp.int32, (block, block), 0)
    for start in range(0, length, block):
        rows = pl.ds(start, block)
        scaled = qkv_ref[rows, :HD] * bf16(1.0 / math.sqrt(HD))
        ones = jnp.ones((block, 3), bf16)
        queries = jnp.concatenate([scaled, ones, jnp.zeros((block, HD - 3), bf16)], axis=1)
        corner = jnp.where(key_id <= row_id, dot_last(queries, k_ref[rows, :]), -jnp.inf)
        top = jnp.max(corner, axis=1, keepdims=True)
        if start:
            scores = dot_last(queries, k_ref[:start, :])
            top = jnp.maximum(top, jnp.max(scores, axis=1, keepdims=True))
        accum = jnp.dot(
            jnp.exp(corner - top).astype(bf16), v_ref[rows, :], preferred_element_type=f32
        )
        if start:
            accum = accum + jnp.dot(
                jnp.exp(scores - top).astype(bf16), v_ref[:start, :], preferred_element_type=f32
            )
        total = accum[:, HD : HD + 1]
        context_ref[rows, :] = (accum[:, :HD] / total).astype(bf16)
        lse = three_parts(-(top + jnp.log(total)))
        q_ref[rows, :] = jnp.concatenate(
            [scaled, ones, *lse, jnp.zeros((block, HD - 6), bf16)], axis=1
        )


def backward_kernel(block, q_ref, k_ref, v_ref, context_ref, grad_ref, out_ref, gk_ref, gv_ref):
    length = q_ref.shape[0]
    row_id = lax.broadcasted_iota(jnp.int32, (block, block), 0)
    query_id = lax.broadcasted_iota(jnp.int32, (block, block), 1)
    for start in range(0, length, block):
        rows = pl.ds(start, block)
        stop = start + block
        queries = q_ref[rows, :]
        grads = grad_ref[rows, :]
        delta = jnp.sum(
            grads.astype(f32) * context_ref[rows, :].astype(f32), axis=1, keepdims=True
        )
        grads = jnp.concatenate(
            [grads, *three_parts(-delta), jnp.zeros((block, HD - 3), bf16)], axis=1
        )
        corner = jnp.where(row_id <= query_id, jnp.exp(dot_last(k_ref[rows, :], queries)), 0.0)
        corner_grad = (corner * dot_last(v_ref[rows, :], grads)).astype(bf16)
        corner = corner.astype(bf16)
        gv_ref[rows, :] = jnp.dot(corner, grads, preferred_element_type=f32)
        gk_ref[rows, :] = jnp.dot(corner_grad, queries, preferred_element_type=f32)
        grad_query = lax.dot_general(
            corner_grad, k_ref[rows, :], (((0,), (0,)), ((), ())), preferred_element_type=f32
        )
        if start:
            probs = jnp.exp(dot_last(k_ref[:start, :], queries))
            probs_grad = (probs * dot_last(v_ref[:start, :], grads)).astype(bf16)
            probs = probs.astype(bf16)
            gv_ref[:start, :] += jnp.dot(probs, grads, preferred_element_type=f32)
            gk_ref[:start, :] += jnp.dot(probs_grad, queries, preferred_element_type=f32)
            grad_query = grad_query + lax.dot_general(
                probs_grad, k_ref[:start, :], (((0,), (0,)), ((), ())), preferred_element_type=f32
            )
        out_ref[rows, :HD] = (grad_query[:, :HD] * (1.0 / math.sqrt(HD))).astype(bf16)
    for start in range(0, length, block):
        rows = pl.ds(start, block)
        out_ref[rows, HD : 2 * HD] = gk_ref[rows, :HD].astype(bf16)
        out_ref[rows, 2 * HD : 3 * HD] = gv_ref[rows, :HD].astype(bf16)


def block_of(length):
    return max(256, length // 8) if length % 256 == 0 else length


def attend_forward(qkv, slope):
    length = qkv.shape[0]
    wide = jax.ShapeDtypeStruct((length, 2 * HD), bf16)
    vmem = pl.BlockSpec(memory_space=pltpu.VMEM)
    return pl.pallas_call(
        functools.partial(forward_kernel, block_of(length)),
        out_shape=(jax.ShapeDtypeStruct((length, HD), bf16), wide, wide, wide),
        in_specs=[vmem, pl.BlockSpec(memory_space=pltpu.SMEM)],
        out_specs=(vmem, vmem, vmem, vmem),
        compiler_params=pltpu.CompilerParams(vmem_limit_bytes=48 * 2**20),
        cost_estimate=pl.CostEstimate(
            flops=length * length * 512, bytes_accessed=length * 2048, transcendentals=length * length // 2
        ),
        name="attend_forward",
    )(qkv, slope.reshape(1))


def attend_backward(queries, keys, values, context, grad_context):
    length = queries.shape[0]
    vmem = pl.BlockSpec(memory_space=pltpu.VMEM)
    return pl.pallas_call(
        functools.partial(backward_kernel, block_of(length)),
        out_shape=jax.ShapeDtypeStruct((length, 3 * HD), bf16),
        in_specs=[vmem] * 5,
        out_specs=vmem,
        scratch_shapes=[pltpu.VMEM((length, 2 * HD), f32), pltpu.VMEM((length, 2 * HD), f32)],
        compiler_params=pltpu.CompilerParams(vmem_limit_bytes=48 * 2**20),
        cost_estimate=pl.CostEstimate(
            flops=length * length * 1280, bytes_accessed=length * 2048, transcendentals=length * length // 2
        ),
        name="attend_backward",
    )(queries, keys, values, context, grad_context)


def gather_rows(rows, axis):
    return lax.all_gather(rows, axis, axis=0, tiled=True)


def gather_sequence(rows):
    return gather_rows(gather_rows(rows, "shard"), "ulysses")


def hop(array, mask, size):
    return lax.ppermute(array, PLANE, [(j, j ^ mask) for j in range(size)])


def gather_plane(rows):
    size = lax.axis_size("batch") * lax.axis_size("ulysses")
    if size != 8:
        return gather_rows(rows, PLANE)
    far = [rows] + [hop(rows, mask, 8) for mask in (2, 4, 6)]
    near = [hop(part, 1, 8) for part in far]
    return jnp.concatenate(far + near, axis=0)


def scatter_plane(make_rows, count):
    size = lax.axis_size("batch") * lax.axis_size("ulysses")
    if size != 8:
        return lax.psum_scatter(make_rows(0, size * count), PLANE, scatter_dimension=0, tiled=True)
    other = hop(make_rows(4 * count, 8 * count).astype(bf16), 1, 8)
    mine = make_rows(0, 4 * count) + other.astype(f32)
    parts = mine.reshape(4, count, -1)
    total = parts[0]
    for place, mask in ((1, 2), (2, 4), (3, 6)):
        total = total + hop(parts[place].astype(bf16), mask, 8).astype(f32)
    return total


def solution(mesh):
    nb, nu, ns = (mesh.shape[name] for name in ALL)
    devices = nb * nu * ns
    group = nu * ns
    plane = nb * nu
    repeat = group // HEADS

    def shards(
        hidden,
        ln1_gain,
        ln1_bias,
        qkv_weight,
        qv_bias,
        out_weight,
        out_bias,
        ln2_gain,
        ln2_bias,
        fc1_weight,
        fc1_bias,
        fc2_weight,
        fc2_bias,
        cotangent,
    ):
        tok = hidden.shape[0]
        depth = qkv_weight.shape[0]
        units = fc1_weight.shape[1] // plane
        head = lax.axis_index(SEQUENCE) // repeat
        plane_index = lax.axis_index(PLANE)

        vectors = (ln1_gain, ln1_bias, qv_bias, out_bias, ln2_gain, ln2_bias, fc1_bias, fc2_bias)
        sizes = [vector.shape[0] for vector in vectors]
        packed = jnp.broadcast_to(jnp.concatenate(vectors)[None], (devices, sum(sizes)))
        packed = lax.all_to_all(packed, ALL, split_axis=0, concat_axis=0, tiled=True)
        whole = []
        offset = 0
        for size in sizes:
            whole.append(packed[:, offset : offset + size].reshape(-1).astype(f32))
            offset += size
        gain_one, shift_one, qv_shift, out_shift, gain_two, shift_two, up_shift, down_shift = whole

        sequence = gather_sequence(hidden)
        w_head = lax.all_to_all(
            jnp.repeat(qkv_weight.reshape(depth, HEADS, 3 * HD), repeat, axis=1).reshape(
                depth, group * 3 * HD
            ),
            SEQUENCE,
            split_axis=1,
            concat_axis=0,
            tiled=True,
        )
        w_head = gather_rows(w_head, "batch")
        w_out = gather_rows(out_weight, ALL)
        w_up = lax.all_to_all(fc1_weight, PLANE, split_axis=1, concat_axis=0, tiled=True)
        w_up = (
            gather_rows(w_up, "shard")
            .reshape(ns, plane, depth, units)
            .transpose(1, 0, 2, 3)
            .reshape(D, units)
        )
        w_down = gather_rows(fc2_weight, "shard")
        grad_plane = gather_plane(cotangent)
        w_qkv = gather_rows(qkv_weight, ALL)

        slope = jnp.exp2(-8.0 * (head.astype(f32) + 1.0) / HEADS)
        normed_one = normalize(sequence.astype(f32), gain_one, shift_one)[0].astype(bf16)
        pair = lax.dynamic_slice_in_dim(qv_shift, head * (2 * HD), 2 * HD)
        shift_head = jnp.concatenate([pair[:HD], jnp.zeros((HD,), f32), pair[HD:]])
        qkv = (jnp.dot(normed_one, w_head, preferred_element_type=f32) + shift_head).astype(bf16)
        context, q_wide, k_wide, v_wide = attend_forward(qkv, slope)
        context_rows = lax.all_to_all(context, SEQUENCE, split_axis=0, concat_axis=1, tiled=True)
        if repeat > 1:
            context_rows = context_rows.reshape(tok, HEADS, repeat, HD)[:, :, 0].reshape(tok, D)

        inputs = hidden.astype(f32)
        attended = inputs + (jnp.dot(context_rows, w_out, preferred_element_type=f32) + out_shift)
        normed_two, unit_two, inv_two = normalize(attended, gain_two, shift_two)
        normed_plane = gather_plane(normed_two.astype(bf16))
        up_slice = lax.dynamic_slice_in_dim(up_shift, plane_index * units, units)
        pre_act = jnp.dot(normed_plane, w_up, preferred_element_type=f32) + up_slice
        activated, slope_act = gelu_both(pre_act)
        activated = activated.astype(bf16)
        grad_act = jnp.einsum("td,fd->tf", grad_plane, w_down, preferred_element_type=f32)
        grad_pre = (grad_act * slope_act).astype(bf16)

        grad_norm_two = scatter_plane(
            lambda start, stop: jnp.einsum(
                "tf,df->td", grad_pre[start:stop], w_up, preferred_element_type=f32
            ),
            tok,
        )
        grad_float = cotangent.astype(f32)
        grad_in_two, grad_gain_two, grad_shift_two = normalize_back(
            grad_norm_two, unit_two, inv_two, gain_two
        )
        grad_attended = grad_float + grad_in_two
        grad_round = grad_attended.astype(bf16)
        grad_context = jnp.einsum(
            "te,de->td", grad_round, w_out, preferred_element_type=f32
        ).astype(bf16)
        if repeat > 1:
            grad_context = jnp.repeat(
                grad_context.reshape(tok, HEADS, HD), repeat, axis=1
            ).reshape(tok, group * HD)
        grad_head = lax.all_to_all(
            grad_context, SEQUENCE, split_axis=1, concat_axis=0, tiled=True
        )
        grad_qkv_head = attend_backward(q_wide, k_wide, v_wide, context, grad_head)

        down = scatter_plane(
            lambda start, stop: jnp.dot(
                activated[start:stop], w_down, preferred_element_type=f32
            ),
            tok,
        )
        output = down + down_shift + attended

        grad_down_w = jnp.einsum("tf,td->fd", activated, grad_plane, preferred_element_type=f32)
        grad_down_w = lax.psum_scatter(
            grad_down_w.astype(bf16), "shard", scatter_dimension=0, tiled=True
        ).astype(f32)
        grad_up_w = jnp.einsum("td,tf->df", normed_plane, grad_pre, preferred_element_type=f32)
        grad_up_w = (
            grad_up_w.astype(bf16)
            .reshape(plane, ns, depth, units)
            .transpose(1, 0, 2, 3)
            .reshape(D, units)
        )
        grad_up_w = lax.psum_scatter(grad_up_w, "shard", scatter_dimension=0, tiled=True)
        grad_up_w = lax.all_to_all(
            grad_up_w, PLANE, split_axis=0, concat_axis=1, tiled=True
        ).astype(f32)
        grad_out_w = jnp.einsum("td,te->de", context_rows, grad_round, preferred_element_type=f32)
        grad_out_w = lax.psum_scatter(
            grad_out_w.astype(bf16), ALL, scatter_dimension=0, tiled=True
        ).astype(f32)

        grad_qkv = lax.all_to_all(
            grad_qkv_head, SEQUENCE, split_axis=0, concat_axis=1, tiled=True
        )
        if repeat > 1:
            grad_qkv = grad_qkv.reshape(tok, HEADS, repeat, 3 * HD)[:, :, 0].reshape(tok, 3 * D)
        grad_qkv_w = jnp.einsum("td,tc->dc", normed_one, grad_qkv_head, preferred_element_type=f32)
        grad_qkv_w = lax.psum_scatter(
            grad_qkv_w.astype(bf16), "batch", scatter_dimension=0, tiled=True
        )
        grad_qkv_w = lax.all_to_all(
            grad_qkv_w, SEQUENCE, split_axis=0, concat_axis=1, tiled=True
        ).astype(f32)
        if repeat > 1:
            grad_qkv_w = grad_qkv_w.reshape(depth, HEADS, repeat, 3 * HD)[:, :, 0].reshape(
                depth, 3 * D
            )
        grad_norm_one = jnp.einsum("te,de->td", grad_qkv, w_qkv, preferred_element_type=f32)
        unit_one, inv_one = normalize(inputs, gain_one, shift_one)[1:]
        grad_in_one, grad_gain_one, grad_shift_one = normalize_back(
            grad_norm_one, unit_one, inv_one, gain_one
        )
        input_grad = grad_attended + grad_in_one

        column_sums = jnp.sum(grad_qkv.astype(f32), axis=0).reshape(HEADS, 3, HD)
        grad_qv = jnp.stack([column_sums[:, 0], column_sums[:, 2]], axis=1).reshape(2 * D)
        grad_up_b = lax.dynamic_update_slice_in_dim(
            jnp.zeros_like(up_shift),
            jnp.sum(grad_pre.astype(f32), axis=0),
            plane_index * units,
            0,
        )
        terms = (
            grad_gain_one,
            grad_shift_one,
            grad_qv,
            jnp.sum(grad_attended, axis=0),
            grad_gain_two,
            grad_shift_two,
            grad_up_b,
            jnp.sum(grad_float, axis=0),
        )
        terms = jnp.concatenate([term.reshape(devices, -1) for term in terms], axis=1)
        terms = lax.all_to_all(terms, ALL, split_axis=0, concat_axis=0, tiled=True)
        terms = jnp.sum(terms, axis=0)
        small = []
        offset = 0
        for size in sizes:
            small.append(terms[offset : offset + size])
            offset += size
        return (
            output,
            input_grad,
            small[0],
            small[1],
            grad_qkv_w,
            small[2],
            grad_out_w,
            small[3],
            small[4],
            small[5],
            grad_up_w,
            small[6],
            grad_down_w,
            small[7],
        )

    rows = P(ALL, None)
    vector = P(ALL)
    return jax.shard_map(
        shards,
        mesh=mesh,
        in_specs=(
            rows,
            vector,
            vector,
            rows,
            vector,
            rows,
            vector,
            vector,
            vector,
            rows,
            vector,
            rows,
            vector,
            rows,
        ),
        out_specs=(
            rows,
            rows,
            vector,
            vector,
            rows,
            vector,
            rows,
            vector,
            vector,
            vector,
            rows,
            vector,
            rows,
            vector,
        ),
        check_vma=False,
    )
```

```python
import functools
import math

import jax
import jax.numpy as jnp
from jax import lax
from jax.experimental import pallas as pl
from jax.experimental.pallas import tpu as pltpu
from jax.sharding import PartitionSpec as P

D = 1024
HEADS = 16
HD = 64

norm_eps = 1e-05
gelu_coef = 0.7978845608028654

ALL = ("batch", "ulysses", "shard")
SEQUENCE = ("ulysses", "shard")
PLANE = ("batch", "ulysses")
bf16 = jnp.bfloat16
f32 = jnp.float32


def normalize(inputs, gain, shift):
    center = jnp.mean(inputs, axis=-1, keepdims=True)
    centred = inputs - center
    variance = jnp.mean(centred * centred, axis=-1, keepdims=True)
    inverse = lax.rsqrt(variance + norm_eps)
    unit_rows = centred * inverse
    return (unit_rows * gain + shift, unit_rows, inverse)


def normalize_back(grad_out, unit_rows, inverse, gain):
    grad_unit = grad_out * gain
    first = jnp.mean(grad_unit, axis=-1, keepdims=True)
    second = jnp.mean(grad_unit * unit_rows, axis=-1, keepdims=True)
    grad_in = inverse * (grad_unit - first - unit_rows * second)
    return (grad_in, jnp.sum(grad_out * unit_rows, axis=0), jnp.sum(grad_out, axis=0))


def gelu_both(pre_act):
    inner = gelu_coef * (pre_act + 0.044715 * pre_act * pre_act * pre_act)
    tanh_val = jnp.tanh(inner)
    value = 0.5 * pre_act * (1.0 + tanh_val)
    slope = 0.5 * (1.0 + tanh_val) + 0.5 * pre_act * (1.0 - tanh_val * tanh_val) * gelu_coef * (
        1.0 + 3.0 * 0.044715 * pre_act * pre_act
    )
    return (value, slope)


def three_parts(column):
    high = column.astype(bf16)
    rest = column - high.astype(f32)
    middle = rest.astype(bf16)
    low = (rest - middle.astype(f32)).astype(bf16)
    return (high, middle, low)


def dot_last(left, right):
    return lax.dot_general(left, right, (((1,), (1,)), ((), ())), preferred_element_type=f32)


def pack_kernel(repeat, stride, weight_ref, vector_ref, out_ref):
    depth = weight_ref.shape[0]
    extra = vector_ref.shape[0]
    width = 3 * HD
    blank = jnp.zeros((stride - depth - extra, width), bf16)
    for place in range(out_ref.shape[0] // stride):
        head = place // repeat
        out_ref[pl.ds(place * stride, stride), :] = jnp.concatenate(
            [weight_ref[:, head * width : (head + 1) * width], vector_ref[...], blank], axis=0
        )


def pack_columns(weight, vectors, group, stride):
    return pl.pallas_call(
        functools.partial(pack_kernel, group // HEADS, stride),
        out_shape=jax.ShapeDtypeStruct((group * stride, 3 * HD), bf16),
        in_specs=[pl.BlockSpec(memory_space=pltpu.VMEM)] * 2,
        out_specs=pl.BlockSpec(memory_space=pltpu.VMEM),
        cost_estimate=pl.CostEstimate(
            flops=0, bytes_accessed=4 * weight.size, transcendentals=0
        ),
        name="pack_columns",
    )(weight, vectors)


def wide_views(wide_ref):
    return [wide_ref.at[:, 2 * HD * part : 2 * HD * (part + 1)] for part in range(4)]


def forward_kernel(block, tok, depth, stride, pieces, lots, *refs):
    piece_refs = refs[:pieces]
    lot_refs = refs[pieces : pieces + lots]
    (
        gain_ref,
        shift_ref,
        head_shift_ref,
        slope_ref,
        place_ref,
        normed_ref,
        turned_ref,
        wide_ref,
        weight_ref,
        qkv_ref,
    ) = refs[pieces + lots :]
    length = normed_ref.shape[0]
    q_ref, k_ref, v_ref, context_ref = wide_views(wide_ref)
    slope = slope_ref[0]
    for lot in range(lots):
        count = lot_refs[lot].shape[0] // stride
        if lots == 2:
            base = pl.multiple_of((place_ref[1] ^ lot) * (count * depth), count * depth)
        else:
            base = lot * count * depth
        for place in range(count):
            weight_ref[pl.ds(base + place * depth, depth), :] = lot_refs[lot][
                pl.ds(place * stride, depth), :
            ]
    gain = gain_ref[...]
    shift = shift_ref[...]
    start = 0
    for piece_ref in piece_refs:
        for first in range(0, piece_ref.shape[0], tok):
            hidden = piece_ref[pl.ds(first, tok), :].astype(f32)
            normed_ref[pl.ds(start, tok), :] = normalize(hidden, gain, shift)[0].astype(bf16)
            start += tok
    for place in range(length // tok):
        target = pl.multiple_of((place_ref[0] ^ place) * tok, tok)
        qkv_ref[pl.ds(target, tok), :] = (
            jnp.dot(
                normed_ref[pl.ds(place * tok, tok), :],
                weight_ref[...],
                preferred_element_type=f32,
            )
            + head_shift_ref[...]
        ).astype(bf16)
    for start in range(0, length, block):
        rows = pl.ds(start, block)
        qkv = qkv_ref[rows, :]
        zeros = jnp.zeros((block, HD - 6), bf16)
        ones = jnp.ones((block, 3), bf16)
        position = start + lax.broadcasted_iota(jnp.int32, (block, 1), 0)
        bias = three_parts(position.astype(f32) * slope)
        k_ref[rows, :] = jnp.concatenate([qkv[:, HD : 2 * HD], *bias, ones, zeros], axis=1)
        v_ref[rows, :] = jnp.concatenate(
            [qkv[:, 2 * HD : 3 * HD], ones, jnp.zeros((block, HD - 3), bf16)], axis=1
        )
    key_id = lax.broadcasted_iota(jnp.int32, (block, block), 1)
    row_id = lax.broadcasted_iota(jnp.int32, (block, block), 0)
    for start in range(0, length, block):
        rows = pl.ds(start, block)
        scaled = qkv_ref[rows, :HD] * bf16(1.0 / math.sqrt(HD))
        ones = jnp.ones((block, 3), bf16)
        queries = jnp.concatenate([scaled, ones, jnp.zeros((block, HD - 3), bf16)], axis=1)
        corner = jnp.where(key_id <= row_id, dot_last(queries, k_ref[rows, :]), -jnp.inf)
        top = jnp.max(corner, axis=1, keepdims=True)
        if start:
            scores = dot_last(queries, k_ref[:start, :])
            top = jnp.maximum(top, jnp.max(scores, axis=1, keepdims=True))
        accum = jnp.dot(
            jnp.exp(corner - top).astype(bf16), v_ref[rows, :], preferred_element_type=f32
        )
        if start:
            accum = accum + jnp.dot(
                jnp.exp(scores - top).astype(bf16), v_ref[:start, :], preferred_element_type=f32
            )
        total = accum[:, HD : HD + 1]
        context = (accum[:, :HD] / total).astype(bf16)
        context_ref[rows, :] = jnp.concatenate([context, jnp.zeros((block, HD), bf16)], axis=1)
        for part in range(block // tok):
            turned_ref[start // tok + part] = context[part * tok : (part + 1) * tok].T
        lse = three_parts(-(top + jnp.log(total)))
        q_ref[rows, :] = jnp.concatenate(
            [scaled, ones, *lse, jnp.zeros((block, HD - 6), bf16)], axis=1
        )


def backward_kernel(
    block,
    tok,
    order_ref,
    wide_ref,
    grad_ref,
    turned_ref,
    mixed_ref,
    gk_ref,
    gv_ref,
    out_ref,
):
    length = wide_ref.shape[0]
    q_ref, k_ref, v_ref, context_ref = wide_views(wide_ref)
    row_id = lax.broadcasted_iota(jnp.int32, (block, block), 0)
    query_id = lax.broadcasted_iota(jnp.int32, (block, block), 1)
    for start in range(0, length, block):
        rows = pl.ds(start, block)
        stop = start + block
        queries = q_ref[rows, :]
        grads = jnp.concatenate(
            [grad_ref[start // tok + part].T for part in range(block // tok)], axis=0
        )
        delta = jnp.sum(
            grads.astype(f32) * context_ref[rows, :HD].astype(f32), axis=1, keepdims=True
        )
        grads = jnp.concatenate(
            [grads, *three_parts(-delta), jnp.zeros((block, HD - 3), bf16)], axis=1
        )
        corner = jnp.where(row_id <= query_id, jnp.exp(dot_last(k_ref[rows, :], queries)), 0.0)
        corner_grad = (corner * dot_last(v_ref[rows, :], grads)).astype(bf16)
        corner = corner.astype(bf16)
        gv_ref[rows, :] = jnp.dot(corner, grads, preferred_element_type=f32)
        gk_ref[rows, :] = jnp.dot(corner_grad, queries, preferred_element_type=f32)
        grad_query = lax.dot_general(
            corner_grad, k_ref[rows, :], (((0,), (0,)), ((), ())), preferred_element_type=f32
        )
        if start:
            probs = jnp.exp(dot_last(k_ref[:start, :], queries))
            probs_grad = (probs * dot_last(v_ref[:start, :], grads)).astype(bf16)
            probs = probs.astype(bf16)
            gv_ref[:start, :] += jnp.dot(probs, grads, preferred_element_type=f32)
            gk_ref[:start, :] += jnp.dot(probs_grad, queries, preferred_element_type=f32)
            grad_query = grad_query + lax.dot_general(
                probs_grad, k_ref[:start, :], (((0,), (0,)), ((), ())), preferred_element_type=f32
            )
        out_ref[rows, :HD] = (grad_query[:, :HD] * (1.0 / math.sqrt(HD))).astype(bf16)
    for start in range(0, length, block):
        rows = pl.ds(start, block)
        out_ref[rows, HD : 2 * HD] = gk_ref[rows, :HD].astype(bf16)
        out_ref[rows, 2 * HD : 3 * HD] = gv_ref[rows, :HD].astype(bf16)
    for place in range(length // tok):
        target = pl.multiple_of((order_ref[0] ^ place) * tok, tok)
        part = out_ref[pl.ds(place * tok, tok), :]
        mixed_ref[pl.ds(target, tok), :] = part
        turned_ref[place] = part.T


def block_of(length):
    return max(256, length // 8) if length % 256 == 0 else length


def attend_forward(pieces, lots, gain, shift, head_shift, slope, place, tok, depth, stride):
    length = sum(piece.shape[0] for piece in pieces)
    vmem = pl.BlockSpec(memory_space=pltpu.VMEM)
    smem = pl.BlockSpec(memory_space=pltpu.SMEM)
    return pl.pallas_call(
        functools.partial(
            forward_kernel, block_of(length), tok, depth, stride, len(pieces), len(lots)
        ),
        out_shape=(
            jax.ShapeDtypeStruct((length, D), bf16),
            jax.ShapeDtypeStruct((length // tok, HD, tok), bf16),
            jax.ShapeDtypeStruct((length, 8 * HD), bf16),
        ),
        in_specs=[vmem] * (len(pieces) + len(lots) + 3) + [smem, smem],
        out_specs=(vmem,) * 3,
        scratch_shapes=[pltpu.VMEM((D, 3 * HD), bf16), pltpu.VMEM((length, 3 * HD), bf16)],
        compiler_params=pltpu.CompilerParams(vmem_limit_bytes=56 * 2**20),
        cost_estimate=pl.CostEstimate(
            flops=length * length * 512 + length * D * 400,
            bytes_accessed=length * D * 4,
            transcendentals=length * length // 2,
        ),
        name="attend_forward",
    )(
        *pieces,
        *lots,
        gain.reshape(1, -1),
        shift.reshape(1, -1),
        head_shift.reshape(1, -1),
        slope.reshape(1),
        place,
    )


def attend_backward(order, wide, grad_context, tok):
    length = wide.shape[0]
    vmem = pl.BlockSpec(memory_space=pltpu.VMEM)
    return pl.pallas_call(
        functools.partial(backward_kernel, block_of(length), tok),
        out_shape=(
            jax.ShapeDtypeStruct((length // tok, 3 * HD, tok), bf16),
            jax.ShapeDtypeStruct((length, 3 * HD), bf16),
        ),
        in_specs=[pl.BlockSpec(memory_space=pltpu.SMEM)] + [vmem] * 2,
        out_specs=(vmem, vmem),
        scratch_shapes=[
            pltpu.VMEM((length, 2 * HD), f32),
            pltpu.VMEM((length, 2 * HD), f32),
            pltpu.VMEM((length, 3 * HD), bf16),
        ],
        compiler_params=pltpu.CompilerParams(vmem_limit_bytes=48 * 2**20),
        cost_estimate=pl.CostEstimate(
            flops=length * length * 1280,
            bytes_accessed=length * 2048,
            transcendentals=length * length // 2,
        ),
        name="attend_backward",
    )(order.reshape(1), wide, grad_context)


RELATIVE = (0, 2, 4, 6, 1, 3, 5, 7)


def dot_first(left, right):
    return lax.dot_general(left, right, (((0,), (0,)), ((), ())), preferred_element_type=f32)


def middle_kernel(tok, depth, *refs):
    normed_refs, grad_refs = refs[:8], refs[8:16]
    lines_ref, shift_ref, act_ref, pre_ref, odd_ref, sum_ref, up_ref, down_ref = refs[16:]
    sums = jnp.zeros(sum_ref.shape, f32)
    units = up_ref.shape[1]
    part = units // 4
    for line in range(4):
        for place in range(8):
            up_ref[pl.ds((place * 4 + line) * depth, depth), :] = lines_ref[
                line, pl.ds(place * depth, depth), :
            ]
        for side in range(D // units):
            down_ref[pl.ds(line * part, part), side * units : (side + 1) * units] = lines_ref[
                line, pl.ds(8 * depth + side * part, part), :
            ]
    for pair in (2, 3, 0, 1):
        rows = pl.ds(2 * pair * tok, 2 * tok)
        normed = jnp.concatenate([ref[...] for ref in normed_refs[2 * pair : 2 * pair + 2]], axis=0)
        grads = jnp.concatenate([ref[...] for ref in grad_refs[2 * pair : 2 * pair + 2]], axis=0)
        pre_act = jnp.dot(normed, up_ref[...], preferred_element_type=f32) + shift_ref[...]
        value, slope = gelu_both(pre_act)
        grad_pre = (dot_last(grads, down_ref[...]) * slope).astype(bf16)
        act_ref[rows, :] = value.astype(bf16)
        pre_ref[rows, :] = grad_pre
        sums = sums + jnp.sum(grad_pre.astype(f32), axis=0, keepdims=True)
        if pair >= 2:
            odd_ref[pl.ds(2 * (pair - 2) * tok, 2 * tok), :] = dot_last(
                grad_pre, up_ref[...]
            ).astype(bf16)
    sum_ref[...] = sums


def weight_kernel(tok, depth, *refs):
    normed_refs, grad_refs = refs[:8], refs[8:16]
    act_ref, pre_ref, place_ref, send_ref, keep_ref, normed_ref, grad_ref, up_ref = refs[16:]
    units = pre_ref.shape[1]
    part = units // 4
    for place in range(8):
        normed_ref[pl.ds(place * tok, tok), :] = normed_refs[place][...]
        grad_ref[pl.ds(place * tok, tok), :] = grad_refs[place][...]
    for start in range(0, D, 256):
        up_ref[pl.ds(start, 256), :] = dot_first(normed_ref[:, start : start + 256], pre_ref[...])
    low = place_ref[0] & 1
    for high in range(2):
        for out_ref, bit in ((send_ref, 1 - low), (keep_ref, low)):
            line = 2 * high + bit
            columns = pl.ds(pl.multiple_of(line * part, part), part)
            out_ref[high, :part, :] = dot_first(act_ref[:, columns], grad_ref[...]).astype(
                out_ref.dtype
            )
            for place, mask in enumerate(RELATIVE):
                source = ((place_ref[1] ^ mask) * 4 + line) * depth
                out_ref[
                    high,
                    part + place % 4 * depth : part + (place % 4 + 1) * depth,
                    place // 4 * units : (place // 4 + 1) * units,
                ] = up_ref[pl.ds(pl.multiple_of(source, depth), depth), :].astype(out_ref.dtype)


def pair_kernel(tok, pre_ref, up_ref, other_ref, own_ref, *part_refs):
    for place in range(4):
        rows = pl.ds(place * tok, tok)
        pair = dot_last(pre_ref[rows, :], up_ref[...]) + other_ref[rows, :].astype(f32)
        out_ref = part_refs[place - 1] if place else own_ref
        out_ref[...] = pair.astype(out_ref.dtype)


def late_kernel(tok, odd, act_ref, down_ref, context_ref, round_ref, place_ref, *refs):
    width = context_ref.shape[0] // 8
    for place in range(4):
        act = act_ref[pl.ds((4 * odd + place) * tok, tok), :]
        rows = jnp.dot(act, down_ref[...], preferred_element_type=f32)
        block = place_ref[1] ^ RELATIVE[4 * odd + place]
        columns = pl.ds(pl.multiple_of(block * width, width), width)
        weight = jnp.dot(context_ref[columns, :], round_ref[...], preferred_element_type=f32)
        first = pl.ds(place * (tok + width), tok)
        second = pl.ds(place * (tok + width) + tok, width)
        if odd:
            refs[0][first, :] = rows.astype(bf16)
            refs[0][second, :] = weight.astype(bf16)
        else:
            out_ref = refs[1 + place]
            out_ref[:tok, :] = (rows + refs[0][first, :].astype(f32)).astype(out_ref.dtype)
            out_ref[tok:, :] = (weight + refs[0][second, :].astype(f32)).astype(out_ref.dtype)


def call_kernel(kernel, name, outs, flops, values, scalars=0, scratch=()):
    vmem = pl.BlockSpec(memory_space=pltpu.VMEM)
    smem = pl.BlockSpec(memory_space=pltpu.SMEM)
    outs = [jax.ShapeDtypeStruct(shape, dtype) for shape, dtype in outs]
    size = sum(value.size * value.dtype.itemsize for value in (*values, *outs))
    return pl.pallas_call(
        kernel,
        out_shape=outs,
        in_specs=[vmem] * (len(values) - scalars) + [smem] * scalars,
        out_specs=[vmem] * len(outs),
        scratch_shapes=[pltpu.VMEM(shape, dtype) for shape, dtype in scratch],
        compiler_params=pltpu.CompilerParams(vmem_limit_bytes=48 * 2**20),
        cost_estimate=pl.CostEstimate(flops=flops, bytes_accessed=size, transcendentals=0),
        name=name,
    )(*values)


def gather_rows(rows, axis):
    return lax.all_gather(rows, axis, axis=0, tiled=True)


def after(values, *others):
    return lax.optimization_barrier((values, others))[0]


def hop(array, axes, mask, size):
    return lax.ppermute(array, axes, [(j, j ^ mask) for j in range(size)])


def gather_sequence(rows):
    if (lax.axis_size("ulysses"), lax.axis_size("shard")) != (4, 4):
        return ([gather_rows(gather_rows(rows, "shard"), "ulysses")], False)
    across = hop(rows, SEQUENCE, 2, 16)
    beside = hop(rows, SEQUENCE, 1, 16)
    side = [hop(rows, SEQUENCE, 8, 16), hop(beside, SEQUENCE, 8, 16)]
    beyond = hop(after(across, side[0]), SEQUENCE, 1, 16)
    line = [rows, beside, across, beyond]
    side += [hop(across, SEQUENCE, 8, 16), hop(after(beyond, side[1]), SEQUENCE, 8, 16)]
    near = [hop(part, SEQUENCE, 4, 16) for part in line]
    far = [hop(part, SEQUENCE, 4, 16) for part in side]
    return (line + near + side + far, True)


def plane_bits():
    index = lax.axis_index(PLANE)
    return [(index >> bit) & 1 for bit in (2, 1, 0)]


def gather_line(rows):
    if lax.axis_size("shard") != 4:
        return gather_rows(rows, "shard")
    across = hop(rows, "shard", 2, 4)
    beside = hop(rows, "shard", 1, 4)
    beyond = hop(across, "shard", 1, 4)
    index = lax.axis_index("shard")
    odd, high = (index & 1) == 1, (index >> 1) == 1
    here = [jnp.where(odd, beside, rows), jnp.where(odd, rows, beside)]
    there = [jnp.where(odd, beyond, across), jnp.where(odd, across, beyond)]
    lower = [jnp.where(high, b, a) for a, b in zip(here, there)]
    upper = [jnp.where(high, a, b) for a, b in zip(here, there)]
    return jnp.concatenate(lower + upper, axis=0)


def send_far(rows):
    if lax.axis_size("batch") * lax.axis_size("ulysses") != 8:
        return [rows]
    return [rows] + [hop(rows, PLANE, mask, 8) for mask in (2, 4, 6)]


def join_near(far):
    if len(far) == 1:
        return [gather_rows(far[0], PLANE)]
    return far + [hop(part, PLANE, 1, 8) for part in far]


def send_parts(own, parts):
    for part, mask in zip(parts, RELATIVE[1:4]):
        own = own + hop(part, PLANE, mask, 8).astype(f32)
    return own


def send_line(rows):
    index = lax.axis_index("shard")
    rows = rows.reshape(2, 2, *rows.shape[1:])
    low = index & 1
    sent = hop(lax.dynamic_index_in_dim(rows, 1 - low, 1, False).astype(bf16), "shard", 1, 4)
    rows = lax.dynamic_index_in_dim(rows, low, 1, False) + sent.astype(f32)
    return send_line_last(rows)


def send_line_last(rows, gate=(), use=()):
    high = lax.axis_index("shard") >> 1
    sent = lax.dynamic_index_in_dim(rows, 1 - high, 0, False).astype(bf16)
    sent = hop(after(sent, gate), "shard", 2, 4)
    return after(lax.dynamic_index_in_dim(rows, high, 0, False), use) + sent.astype(f32)


def from_relative(blocks):
    shape = blocks.shape
    blocks = jnp.moveaxis(blocks.reshape(2, 2, 2, *shape[1:]), 0, 2)
    for axis, bit in enumerate(plane_bits()):
        blocks = jnp.where(bit == 1, jnp.flip(blocks, axis), blocks)
    return blocks.reshape(shape)


def exchange_plane(blocks):
    near = hop(blocks[4:], PLANE, 1, 8)
    own, other = [blocks[0]], [near[0]]
    for place, mask in ((1, 2), (2, 4), (3, 6)):
        pair = hop(jnp.stack([blocks[place], near[place]]), PLANE, mask, 8)
        own.append(pair[0])
        other.append(pair[1])
    return from_relative(jnp.stack(own + other))


def solution(mesh):
    nb, nu, ns = (mesh.shape[name] for name in ALL)
    devices = nb * nu * ns
    group = nu * ns
    plane = nb * nu
    repeat = group // HEADS
    cube = plane == 8 and ns == 4

    def shards(
        hidden,
        ln1_gain,
        ln1_bias,
        qkv_weight,
        qv_bias,
        out_weight,
        out_bias,
        ln2_gain,
        ln2_bias,
        fc1_weight,
        fc1_bias,
        fc2_weight,
        fc2_bias,
        cotangent,
    ):
        tok = hidden.shape[0]
        depth = qkv_weight.shape[0]
        units = fc1_weight.shape[1] // plane
        head = lax.axis_index(SEQUENCE) // repeat
        plane_index = lax.axis_index(PLANE)

        vectors = (ln1_gain, ln1_bias, qv_bias, out_bias, ln2_gain, ln2_bias, fc1_bias, fc2_bias)
        sizes = [vector.shape[0] for vector in vectors]
        extra = -(-sum(sizes) // (3 * HD))
        stride = -(-(depth + extra) // 16) * 16
        packed = 0
        for place, vector in enumerate(vectors):
            before = sum(sizes[:place])
            after_it = extra * 3 * HD - before - vector.shape[0]
            packed = packed + jnp.pad(vector, (before, after_it))
        columns = pack_columns(qkv_weight, packed.reshape(extra, 3 * HD), group, stride)
        columns = lax.all_to_all(columns, SEQUENCE, split_axis=0, concat_axis=0, tiled=True)
        grad_far = send_far(cotangent)
        pieces, mixed = gather_sequence(after(hidden, columns, grad_far))
        joined = gather_rows(jnp.concatenate([out_weight, qkv_weight], axis=1), ALL)
        w_out, w_qkv = joined[:, :D], joined[:, D:]
        batch = lax.axis_index("batch")
        if nb == 2:
            lots = [columns, hop(columns, "batch", 1, 2)]
        else:
            lots = list(jnp.split(gather_rows(columns, "batch"), nb))
        packed = jnp.stack([lot.reshape(group, stride, 3 * HD)[:, depth:depth + extra] for lot in lots])
        if nb == 2:
            packed = jnp.where(batch == 0, packed, packed[::-1])
        packed = packed.reshape(devices, extra * 3 * HD)
        whole = []
        offset = 0
        for size in sizes:
            whole.append(packed[:, offset : offset + size].reshape(-1).astype(f32))
            offset += size
        gain_one, shift_one, qv_shift, out_shift, gain_two, shift_two, up_shift, down_shift = whole

        w_up = lax.all_to_all(
            after(fc1_weight, pieces[-1]), PLANE, split_axis=1, concat_axis=0, tiled=True
        )

        slope = jnp.exp2(-8.0 * (head.astype(f32) + 1.0) / HEADS)
        pair = lax.dynamic_slice_in_dim(qv_shift, head * (2 * HD), 2 * HD)
        shift_head = jnp.concatenate([pair[:HD], jnp.zeros((HD,), f32), pair[HD:]])
        order = lax.axis_index(SEQUENCE) if mixed else jnp.zeros((), jnp.int32)
        normed_one, context, wide = attend_forward(
            pieces,
            lots,
            gain_one,
            shift_one,
            shift_head,
            slope,
            jnp.stack([order, batch]),
            tok,
            depth,
            stride,
        )
        context, w_up = lax.optimization_barrier((context, w_up))
        grad_plane = join_near(grad_far)
        sides = [fc2_weight[:, start : start + units] for start in range(0, D, units)]
        lines = gather_rows(jnp.concatenate([w_up, *sides], axis=0), "shard")
        lines = lines.reshape(ns, -1, units)
        turned = lax.all_to_all(context, SEQUENCE, split_axis=0, concat_axis=0, tiled=True)
        turned = turned.reshape(HEADS, repeat, HD, tok)[:, 0].reshape(D, tok)
        turned, w_out = lax.optimization_barrier((turned, w_out))

        inputs = hidden.astype(f32)
        attended = inputs + (dot_first(turned, w_out) + out_shift)
        normed_two, unit_two, inv_two = normalize(attended, gain_two, shift_two)
        normed_plane = join_near(send_far(normed_two.astype(bf16)))
        up_slice = lax.dynamic_slice_in_dim(up_shift, plane_index * units, units)
        place = jnp.stack([lax.axis_index("shard"), plane_index])
        if cube:
            flops = 2 * plane * tok * D * units
            activated, grad_pre, odd, grad_up_b, w_up, w_down = call_kernel(
                functools.partial(middle_kernel, tok, depth),
                "middle",
                [
                    ((plane * tok, units), bf16),
                    ((plane * tok, units), bf16),
                    ((plane // 2 * tok, D), bf16),
                    ((1, units), f32),
                    ((D, units), bf16),
                    ((units, D), bf16),
                ],
                flops * 5 // 2,
                [*normed_plane, *grad_plane, lines, up_slice.reshape(1, units)],
            )
            other = hop(odd, PLANE, 1, 8)
            own, *parts = call_kernel(
                functools.partial(pair_kernel, tok),
                "pair_sums",
                [((tok, D), f32)] + [((tok, D), bf16)] * 3,
                flops // 2,
                [grad_pre, w_up, other],
            )
            grad_norm_two = send_parts(own, parts)
            block = (2, units // ns + plane // 2 * depth, D)
            line_send, line_keep = call_kernel(
                functools.partial(weight_kernel, tok, depth),
                "weight_grads",
                [(block, bf16), (block, f32)],
                flops * 2,
                [*normed_plane, *grad_plane, *after((activated, grad_pre), own), place],
                1,
                [((plane * tok, D), bf16), ((plane * tok, D), bf16), ((D, units), f32)],
            )
            line_sent = hop(line_send, "shard", 1, 4)
        else:
            (normed_plane,), (grad_plane,) = normed_plane, grad_plane
            w_up = lines[:, : plane * depth].reshape(ns, plane, depth, units)
            w_up = w_up.transpose(1, 0, 2, 3).reshape(D, units)
            w_down = lines[:, plane * depth :].reshape(ns, -1, units // ns, units)
            w_down = w_down.transpose(0, 2, 1, 3).reshape(units, D)
            pre_act = jnp.dot(normed_plane, w_up, preferred_element_type=f32) + up_slice
            activated, slope_act = gelu_both(pre_act)
            activated = activated.astype(bf16)
            grad_act = jnp.einsum("td,fd->tf", grad_plane, w_down, preferred_element_type=f32)
            grad_pre = (grad_act * slope_act).astype(bf16)
            grad_up_b = jnp.sum(grad_pre.astype(f32), axis=0)
            grad_norm_two = jnp.einsum("tf,df->td", grad_pre, w_up, preferred_element_type=f32)
            grad_norm_two = lax.psum_scatter(grad_norm_two, PLANE, scatter_dimension=0, tiled=True)
        grad_float = cotangent.astype(f32)
        grad_in_two, grad_gain_two, grad_shift_two = normalize_back(
            grad_norm_two, unit_two, inv_two, gain_two
        )
        grad_attended = grad_float + grad_in_two
        grad_round = grad_attended.astype(bf16)
        grad_context = dot_last(w_out, grad_round).astype(bf16).reshape(HEADS, HD, tok)
        grad_head = lax.all_to_all(
            jnp.repeat(grad_context, repeat, axis=0),
            SEQUENCE,
            split_axis=0,
            concat_axis=0,
            tiled=True,
        )
        if cube:
            late = (activated, w_down, turned, after(grad_round, grad_context), place)
            both = tok + D // plane
            (odd,) = call_kernel(
                functools.partial(late_kernel, tok, 1),
                "late_odd",
                [((plane // 2 * both, D), bf16)],
                flops // 2 + tok * D * D,
                late,
                1,
            )
            other = hop(odd, PLANE, 1, 8)
            line_sent = after(line_sent, grad_context)
            line = line_keep + line_sent.astype(f32)
            grad_head, line_sent = lax.optimization_barrier((grad_head, line_sent))
        grad_qkv_head, grad_qkv_mixed = attend_backward(
            order, wide, grad_head, tok
        )
        if cube:
            own, *parts = call_kernel(
                lambda act, down, head, turned, more, index, *outs: late_kernel(
                    tok, 0, act, down, head, turned, index, more, *outs
                ),
                "late_even",
                [((both, D), f32)] + [((both, D), bf16)] * 3,
                flops // 2 + tok * D * D,
                (*late[:4], after(other, grad_qkv_head), place),
                1,
            )


        grad_qkv = lax.all_to_all(
            grad_qkv_head, SEQUENCE, split_axis=0, concat_axis=0, tiled=True
        )
        if cube:
            grad_qkv, own = lax.optimization_barrier((grad_qkv, own))
        grad_qkv = grad_qkv.reshape(HEADS, repeat, 3 * HD, tok)[:, 0].reshape(3 * D, tok)
        grad_qkv_w = jnp.einsum(
            "td,tc->dc", normed_one, grad_qkv_mixed, preferred_element_type=f32
        )
        if nb == 2:
            half = D // 2
            kept = lax.axis_index("batch")
            other = lax.dynamic_slice_in_dim(grad_qkv_w, (1 - kept) * half, half).astype(bf16)
            other = hop(other, "batch", 1, 2)
            grad_qkv_w = lax.dynamic_slice_in_dim(
                grad_qkv_w, kept * half, half
            ) + other.astype(f32)
        else:
            grad_qkv_w = lax.psum_scatter(grad_qkv_w, "batch", scatter_dimension=0, tiled=True)
        grad_norm_one = jnp.einsum("et,de->td", grad_qkv, w_qkv, preferred_element_type=f32)
        unit_one, inv_one = normalize(inputs, gain_one, shift_one)[1:]
        grad_in_one, grad_gain_one, grad_shift_one = normalize_back(
            grad_norm_one, unit_one, inv_one, gain_one
        )
        input_grad = grad_attended + grad_in_one

        column_sums = jnp.sum(grad_qkv.astype(f32), axis=1).reshape(HEADS, 3, HD)
        grad_qv = jnp.stack([column_sums[:, 0], column_sums[:, 2]], axis=1).reshape(2 * D)
        grad_up_b = lax.dynamic_update_slice_in_dim(
            jnp.zeros_like(up_shift),
            grad_up_b.reshape(units),
            plane_index * units,
            0,
        )
        terms = (
            grad_gain_one,
            grad_shift_one,
            grad_qv,
            jnp.sum(grad_attended, axis=0),
            grad_gain_two,
            grad_shift_two,
            grad_up_b,
            jnp.sum(grad_float, axis=0),
        )
        terms = jnp.concatenate([term.reshape(devices, -1) for term in terms], axis=1)
        terms = lax.all_to_all(terms, ALL, split_axis=0, concat_axis=0, tiled=True)
        terms = jnp.sum(terms, axis=0)
        if cube:
            both = send_parts(after(own, terms), parts)
            line = send_line_last(line, grad_norm_one, terms)
            down = both[:tok]
            grad_out_w = send_line(both[tok:].reshape(ns, depth, D))
            part = units // ns
            grad_down_w = line[:part]
            grad_up_w = (
                line[part:].astype(bf16).reshape(4, depth, 2, units).transpose(2, 0, 1, 3)
            ).reshape(plane, depth, units)
            grad_up_w = exchange_plane(after(grad_up_w, grad_norm_one))
            grad_up_w = grad_up_w.transpose(1, 0, 2).reshape(depth, plane * units).astype(f32)
        else:
            down = lax.psum_scatter(
                jnp.dot(activated, w_down, preferred_element_type=f32),
                PLANE,
                scatter_dimension=0,
                tiled=True,
            )
            grad_down_w = lax.psum_scatter(
                jnp.einsum("tf,td->fd", activated, grad_plane, preferred_element_type=f32),
                "shard",
                scatter_dimension=0,
                tiled=True,
            )
            grad_up_w = jnp.einsum(
                "td,tf->df", normed_plane, grad_pre, preferred_element_type=f32
            )
            grad_up_w = grad_up_w.reshape(plane, ns, depth, units).transpose(1, 0, 2, 3)
            grad_up_w = lax.psum_scatter(
                grad_up_w.reshape(D, units), "shard", scatter_dimension=0, tiled=True
            )
            grad_up_w = lax.all_to_all(grad_up_w, PLANE, split_axis=0, concat_axis=1, tiled=True)
            grad_out_w = jnp.einsum(
                "dt,te->de", turned, grad_round, preferred_element_type=f32
            )
            grad_out_w = lax.psum_scatter(grad_out_w, ALL, scatter_dimension=0, tiled=True)
        grad_qkv_w = lax.all_to_all(
            after(grad_qkv_w.astype(bf16), grad_norm_one),
            SEQUENCE,
            split_axis=0,
            concat_axis=1,
            tiled=True,
        )
        grad_qkv_w = after(grad_qkv_w, grad_up_w, grad_out_w).astype(f32)
        if repeat > 1:
            grad_qkv_w = grad_qkv_w.reshape(depth, HEADS, repeat, 3 * HD)[:, :, 0].reshape(
                depth, 3 * D
            )
        output = down + down_shift + attended
        small = []
        offset = 0
        for size in sizes:
            small.append(terms[offset : offset + size])
            offset += size
        return (
            output,
            input_grad,
            small[0],
            small[1],
            grad_qkv_w,
            small[2],
            grad_out_w,
            small[3],
            small[4],
            small[5],
            grad_up_w,
            small[6],
            grad_down_w,
            small[7],
        )

    rows = P(ALL, None)
    vector = P(ALL)
    return jax.shard_map(
        shards,
        mesh=mesh,
        in_specs=(
            rows,
            vector,
            vector,
            rows,
            vector,
            rows,
            vector,
            vector,
            vector,
            rows,
            vector,
            rows,
            vector,
            rows,
        ),
        out_specs=(
            rows,
            rows,
            vector,
            vector,
            rows,
            vector,
            rows,
            vector,
            vector,
            vector,
            rows,
            vector,
            rows,
            vector,
        ),
        check_vma=False,
    )
```

```python
import functools
import math

import jax
import jax.numpy as jnp
from jax import lax
from jax.experimental import pallas as pl
from jax.experimental.pallas import tpu as pltpu
from jax.sharding import PartitionSpec as P

D = 1024
HEADS = 16
HD = 64

norm_eps = 1e-05
gelu_coef = 0.7978845608028654

ALL = ("batch", "ulysses", "shard")
SEQUENCE = ("ulysses", "shard")
PLANE = ("batch", "ulysses")
bf16 = jnp.bfloat16
f32 = jnp.float32


def normalize(inputs, gain, shift):
    center = jnp.mean(inputs, axis=-1, keepdims=True)
    centred = inputs - center
    variance = jnp.mean(centred * centred, axis=-1, keepdims=True)
    inverse = lax.rsqrt(variance + norm_eps)
    unit_rows = centred * inverse
    return (unit_rows * gain + shift, unit_rows, inverse)


def normalize_back(grad_out, unit_rows, inverse, gain):
    grad_unit = grad_out * gain
    first = jnp.mean(grad_unit, axis=-1, keepdims=True)
    second = jnp.mean(grad_unit * unit_rows, axis=-1, keepdims=True)
    grad_in = inverse * (grad_unit - first - unit_rows * second)
    return (grad_in, jnp.sum(grad_out * unit_rows, axis=0), jnp.sum(grad_out, axis=0))


def gelu_both(pre_act):
    inner = gelu_coef * (pre_act + 0.044715 * pre_act * pre_act * pre_act)
    tanh_val = jnp.tanh(inner)
    value = 0.5 * pre_act * (1.0 + tanh_val)
    slope = 0.5 * (1.0 + tanh_val) + 0.5 * pre_act * (1.0 - tanh_val * tanh_val) * gelu_coef * (
        1.0 + 3.0 * 0.044715 * pre_act * pre_act
    )
    return (value, slope)


def three_parts(column):
    high = column.astype(bf16)
    rest = column - high.astype(f32)
    middle = rest.astype(bf16)
    low = (rest - middle.astype(f32)).astype(bf16)
    return (high, middle, low)


def dot_last(left, right):
    return lax.dot_general(left, right, (((1,), (1,)), ((), ())), preferred_element_type=f32)


def pack_kernel(repeat, stride, weight_ref, vector_ref, out_ref):
    depth = weight_ref.shape[0]
    extra = vector_ref.shape[0]
    width = 3 * HD
    blank = jnp.zeros((stride - depth - extra, width), bf16)
    for place in range(out_ref.shape[0] // stride):
        head = place // repeat
        out_ref[pl.ds(place * stride, stride), :] = jnp.concatenate(
            [weight_ref[:, head * width : (head + 1) * width], vector_ref[...], blank], axis=0
        )


def pack_columns(weight, vectors, group, stride):
    return pl.pallas_call(
        functools.partial(pack_kernel, group // HEADS, stride),
        out_shape=jax.ShapeDtypeStruct((group * stride, 3 * HD), bf16),
        in_specs=[pl.BlockSpec(memory_space=pltpu.VMEM)] * 2,
        out_specs=pl.BlockSpec(memory_space=pltpu.VMEM),
        cost_estimate=pl.CostEstimate(
            flops=0, bytes_accessed=4 * weight.size, transcendentals=0
        ),
        name="pack_columns",
    )(weight, vectors)


def wide_views(wide_ref):
    return [wide_ref.at[:, 2 * HD * part : 2 * HD * (part + 1)] for part in range(4)]


def forward_kernel(block, tok, depth, stride, pieces, lots, *refs):
    piece_refs = refs[:pieces]
    lot_refs = refs[pieces : pieces + lots]
    (
        gain_ref,
        shift_ref,
        head_shift_ref,
        slope_ref,
        place_ref,
        normed_ref,
        turned_ref,
        wide_ref,
        weight_ref,
        qkv_ref,
    ) = refs[pieces + lots :]
    length = normed_ref.shape[0]
    q_ref, k_ref, v_ref, context_ref = wide_views(wide_ref)
    slope = slope_ref[0]
    for lot in range(lots):
        count = lot_refs[lot].shape[0] // stride
        if lots == 2:
            base = pl.multiple_of((place_ref[1] ^ lot) * (count * depth), count * depth)
        else:
            base = lot * count * depth
        for place in range(count):
            weight_ref[pl.ds(base + place * depth, depth), :] = lot_refs[lot][
                pl.ds(place * stride, depth), :
            ]
    gain = gain_ref[...]
    shift = shift_ref[...]
    start = 0
    for piece_ref in piece_refs:
        for first in range(0, piece_ref.shape[0], tok):
            hidden = piece_ref[pl.ds(first, tok), :].astype(f32)
            normed_ref[pl.ds(start, tok), :] = normalize(hidden, gain, shift)[0].astype(bf16)
            start += tok
    for place in range(length // tok):
        target = pl.multiple_of((place_ref[0] ^ place) * tok, tok)
        qkv_ref[pl.ds(target, tok), :] = (
            jnp.dot(
                normed_ref[pl.ds(place * tok, tok), :],
                weight_ref[...],
                preferred_element_type=f32,
            )
            + head_shift_ref[...]
        ).astype(bf16)
    for start in range(0, length, block):
        rows = pl.ds(start, block)
        qkv = qkv_ref[rows, :]
        zeros = jnp.zeros((block, HD - 6), bf16)
        ones = jnp.ones((block, 3), bf16)
        position = start + lax.broadcasted_iota(jnp.int32, (block, 1), 0)
        bias = three_parts(position.astype(f32) * slope)
        k_ref[rows, :] = jnp.concatenate([qkv[:, HD : 2 * HD], *bias, ones, zeros], axis=1)
        v_ref[rows, :] = jnp.concatenate(
            [qkv[:, 2 * HD : 3 * HD], ones, jnp.zeros((block, HD - 3), bf16)], axis=1
        )
    key_id = lax.broadcasted_iota(jnp.int32, (block, block), 1)
    row_id = lax.broadcasted_iota(jnp.int32, (block, block), 0)
    for start in range(0, length, block):
        rows = pl.ds(start, block)
        scaled = qkv_ref[rows, :HD] * bf16(1.0 / math.sqrt(HD))
        ones = jnp.ones((block, 3), bf16)
        queries = jnp.concatenate([scaled, ones, jnp.zeros((block, HD - 3), bf16)], axis=1)
        corner = jnp.where(key_id <= row_id, dot_last(queries, k_ref[rows, :]), -jnp.inf)
        top = jnp.max(corner, axis=1, keepdims=True)
        if start:
            scores = dot_last(queries, k_ref[:start, :])
            top = jnp.maximum(top, jnp.max(scores, axis=1, keepdims=True))
        accum = jnp.dot(
            jnp.exp(corner - top).astype(bf16), v_ref[rows, :], preferred_element_type=f32
        )
        if start:
            accum = accum + jnp.dot(
                jnp.exp(scores - top).astype(bf16), v_ref[:start, :], preferred_element_type=f32
            )
        total = accum[:, HD : HD + 1]
        context = (accum[:, :HD] / total).astype(bf16)
        context_ref[rows, :] = jnp.concatenate([context, jnp.zeros((block, HD), bf16)], axis=1)
        for part in range(block // tok):
            turned_ref[start // tok + part] = context[part * tok : (part + 1) * tok].T
        lse = three_parts(-(top + jnp.log(total)))
        q_ref[rows, :] = jnp.concatenate(
            [scaled, ones, *lse, jnp.zeros((block, HD - 6), bf16)], axis=1
        )


def backward_kernel(
    block,
    tok,
    order_ref,
    wide_ref,
    grad_ref,
    turned_ref,
    mixed_ref,
    gk_ref,
    gv_ref,
    out_ref,
):
    length = wide_ref.shape[0]
    q_ref, k_ref, v_ref, context_ref = wide_views(wide_ref)
    row_id = lax.broadcasted_iota(jnp.int32, (block, block), 0)
    query_id = lax.broadcasted_iota(jnp.int32, (block, block), 1)
    for start in range(0, length, block):
        rows = pl.ds(start, block)
        stop = start + block
        queries = q_ref[rows, :]
        grads = jnp.concatenate(
            [grad_ref[start // tok + part].T for part in range(block // tok)], axis=0
        )
        delta = jnp.sum(
            grads.astype(f32) * context_ref[rows, :HD].astype(f32), axis=1, keepdims=True
        )
        grads = jnp.concatenate(
            [grads, *three_parts(-delta), jnp.zeros((block, HD - 3), bf16)], axis=1
        )
        corner = jnp.where(row_id <= query_id, jnp.exp(dot_last(k_ref[rows, :], queries)), 0.0)
        corner_grad = (corner * dot_last(v_ref[rows, :], grads)).astype(bf16)
        corner = corner.astype(bf16)
        gv_ref[rows, :] = jnp.dot(corner, grads, preferred_element_type=f32)
        gk_ref[rows, :] = jnp.dot(corner_grad, queries, preferred_element_type=f32)
        grad_query = lax.dot_general(
            corner_grad, k_ref[rows, :], (((0,), (0,)), ((), ())), preferred_element_type=f32
        )
        if start:
            probs = jnp.exp(dot_last(k_ref[:start, :], queries))
            probs_grad = (probs * dot_last(v_ref[:start, :], grads)).astype(bf16)
            probs = probs.astype(bf16)
            gv_ref[:start, :] += jnp.dot(probs, grads, preferred_element_type=f32)
            gk_ref[:start, :] += jnp.dot(probs_grad, queries, preferred_element_type=f32)
            grad_query = grad_query + lax.dot_general(
                probs_grad, k_ref[:start, :], (((0,), (0,)), ((), ())), preferred_element_type=f32
            )
        out_ref[rows, :HD] = (grad_query[:, :HD] * (1.0 / math.sqrt(HD))).astype(bf16)
    for start in range(0, length, block):
        rows = pl.ds(start, block)
        out_ref[rows, HD : 2 * HD] = gk_ref[rows, :HD].astype(bf16)
        out_ref[rows, 2 * HD : 3 * HD] = gv_ref[rows, :HD].astype(bf16)
    for place in range(length // tok):
        target = pl.multiple_of((order_ref[0] ^ place) * tok, tok)
        part = out_ref[pl.ds(place * tok, tok), :]
        mixed_ref[pl.ds(target, tok), :] = part
        turned_ref[place] = part.T


def block_of(length):
    return max(256, length // 8) if length % 256 == 0 else length


def attend_forward(pieces, lots, gain, shift, head_shift, slope, place, tok, depth, stride):
    length = sum(piece.shape[0] for piece in pieces)
    vmem = pl.BlockSpec(memory_space=pltpu.VMEM)
    smem = pl.BlockSpec(memory_space=pltpu.SMEM)
    return pl.pallas_call(
        functools.partial(
            forward_kernel, block_of(length), tok, depth, stride, len(pieces), len(lots)
        ),
        out_shape=(
            jax.ShapeDtypeStruct((length, D), bf16),
            jax.ShapeDtypeStruct((length // tok, HD, tok), bf16),
            jax.ShapeDtypeStruct((length, 8 * HD), bf16),
        ),
        in_specs=[vmem] * (len(pieces) + len(lots) + 3) + [smem, smem],
        out_specs=(vmem,) * 3,
        scratch_shapes=[pltpu.VMEM((D, 3 * HD), bf16), pltpu.VMEM((length, 3 * HD), bf16)],
        compiler_params=pltpu.CompilerParams(vmem_limit_bytes=56 * 2**20),
        cost_estimate=pl.CostEstimate(
            flops=length * length * 512 + length * D * 400,
            bytes_accessed=length * D * 4,
            transcendentals=length * length // 2,
        ),
        name="attend_forward",
    )(
        *pieces,
        *lots,
        gain.reshape(1, -1),
        shift.reshape(1, -1),
        head_shift.reshape(1, -1),
        slope.reshape(1),
        place,
    )


def attend_backward(order, wide, grad_context, tok):
    length = wide.shape[0]
    vmem = pl.BlockSpec(memory_space=pltpu.VMEM)
    return pl.pallas_call(
        functools.partial(backward_kernel, block_of(length), tok),
        out_shape=(
            jax.ShapeDtypeStruct((length // tok, 3 * HD, tok), bf16),
            jax.ShapeDtypeStruct((length, 3 * HD), bf16),
        ),
        in_specs=[pl.BlockSpec(memory_space=pltpu.SMEM)] + [vmem] * 2,
        out_specs=(vmem, vmem),
        scratch_shapes=[
            pltpu.VMEM((length, 2 * HD), f32),
            pltpu.VMEM((length, 2 * HD), f32),
            pltpu.VMEM((length, 3 * HD), bf16),
        ],
        compiler_params=pltpu.CompilerParams(vmem_limit_bytes=48 * 2**20),
        cost_estimate=pl.CostEstimate(
            flops=length * length * 1280,
            bytes_accessed=length * 2048,
            transcendentals=length * length // 2,
        ),
        name="attend_backward",
    )(order.reshape(1), wide, grad_context)


RELATIVE = (0, 2, 4, 6, 1, 3, 5, 7)


def dot_first(left, right):
    return lax.dot_general(left, right, (((0,), (0,)), ((), ())), preferred_element_type=f32)


def middle_kernel(tok, depth, *refs):
    normed_refs, grad_refs = refs[:8], refs[8:16]
    lines_ref, shift_ref, act_ref, pre_ref, odd_ref, sum_ref, up_ref, down_ref = refs[16:]
    sums = jnp.zeros(sum_ref.shape, f32)
    units = up_ref.shape[1]
    part = units // 4
    for line in range(4):
        for place in range(8):
            up_ref[pl.ds((place * 4 + line) * depth, depth), :] = lines_ref[
                line, pl.ds(place * depth, depth), :
            ]
        for side in range(D // units):
            down_ref[pl.ds(line * part, part), side * units : (side + 1) * units] = lines_ref[
                line, pl.ds(8 * depth + side * part, part), :
            ]
    for pair in (2, 3, 0, 1):
        rows = pl.ds(2 * pair * tok, 2 * tok)
        normed = jnp.concatenate([ref[...] for ref in normed_refs[2 * pair : 2 * pair + 2]], axis=0)
        grads = jnp.concatenate([ref[...] for ref in grad_refs[2 * pair : 2 * pair + 2]], axis=0)
        pre_act = jnp.dot(normed, up_ref[...], preferred_element_type=f32) + shift_ref[...]
        value, slope = gelu_both(pre_act)
        grad_pre = (dot_last(grads, down_ref[...]) * slope).astype(bf16)
        act_ref[rows, :] = value.astype(bf16)
        pre_ref[rows, :] = grad_pre
        sums = sums + jnp.sum(grad_pre.astype(f32), axis=0, keepdims=True)
        if pair >= 2:
            odd_ref[pl.ds(2 * (pair - 2) * tok, 2 * tok), :] = dot_last(
                grad_pre, up_ref[...]
            ).astype(bf16)
    sum_ref[...] = sums


def weight_kernel(tok, depth, *refs):
    normed_refs, grad_refs = refs[:8], refs[8:16]
    act_ref, pre_ref, place_ref, *out_refs = refs[16:23]
    normed_ref, grad_ref, up_ref = refs[23:]
    units = pre_ref.shape[1]
    part = units // 4
    for place in range(8):
        normed_ref[pl.ds(place * tok, tok), :] = normed_refs[place][...]
        grad_ref[pl.ds(place * tok, tok), :] = grad_refs[place][...]
    for start in range(0, D, 256):
        up_ref[pl.ds(start, 256), :] = dot_first(normed_ref[:, start : start + 256], pre_ref[...])
    low = place_ref[0] & 1
    for high in range(2):
        for (first_ref, second_ref), bit in ((out_refs[:2], 1 - low), (out_refs[2:], low)):
            line = 2 * high + bit
            columns = pl.ds(pl.multiple_of(line * part, part), part)
            first_ref[high] = dot_first(act_ref[:, columns], grad_ref[...]).astype(first_ref.dtype)
            for place, mask in enumerate(RELATIVE):
                source = ((place_ref[1] ^ mask) * 4 + line) * depth
                second_ref[
                    high,
                    place % 4 * depth : (place % 4 + 1) * depth,
                    place // 4 * units : (place // 4 + 1) * units,
                ] = up_ref[pl.ds(pl.multiple_of(source, depth), depth), :].astype(second_ref.dtype)


def pair_kernel(tok, pre_ref, up_ref, other_ref, own_ref, *part_refs):
    for place in range(4):
        rows = pl.ds(place * tok, tok)
        pair = dot_last(pre_ref[rows, :], up_ref[...]) + other_ref[rows, :].astype(f32)
        out_ref = part_refs[place - 1] if place else own_ref
        out_ref[...] = pair.astype(out_ref.dtype)


def late_kernel(tok, odd, act_ref, down_ref, context_ref, round_ref, place_ref, *refs):
    width = context_ref.shape[0] // 8
    for place in range(4):
        act = act_ref[pl.ds((4 * odd + place) * tok, tok), :]
        rows = jnp.dot(act, down_ref[...], preferred_element_type=f32)
        block = place_ref[1] ^ RELATIVE[4 * odd + place]
        columns = pl.ds(pl.multiple_of(block * width, width), width)
        weight = jnp.dot(context_ref[columns, :], round_ref[...], preferred_element_type=f32)
        first = pl.ds(place * (tok + width), tok)
        second = pl.ds(place * (tok + width) + tok, width)
        if odd:
            refs[0][first, :] = rows.astype(bf16)
            refs[0][second, :] = weight.astype(bf16)
        else:
            out_ref = refs[1 + place]
            out_ref[:tok, :] = (rows + refs[0][first, :].astype(f32)).astype(out_ref.dtype)
            out_ref[tok:, :] = (weight + refs[0][second, :].astype(f32)).astype(out_ref.dtype)


def call_kernel(kernel, name, outs, flops, values, scalars=0, scratch=()):
    vmem = pl.BlockSpec(memory_space=pltpu.VMEM)
    smem = pl.BlockSpec(memory_space=pltpu.SMEM)
    outs = [jax.ShapeDtypeStruct(shape, dtype) for shape, dtype in outs]
    size = sum(value.size * value.dtype.itemsize for value in (*values, *outs))
    return pl.pallas_call(
        kernel,
        out_shape=outs,
        in_specs=[vmem] * (len(values) - scalars) + [smem] * scalars,
        out_specs=[vmem] * len(outs),
        scratch_shapes=[pltpu.VMEM(shape, dtype) for shape, dtype in scratch],
        compiler_params=pltpu.CompilerParams(vmem_limit_bytes=48 * 2**20),
        cost_estimate=pl.CostEstimate(flops=flops, bytes_accessed=size, transcendentals=0),
        name=name,
    )(*values)


def gather_rows(rows, axis):
    return lax.all_gather(rows, axis, axis=0, tiled=True)


def after(values, *others):
    return lax.optimization_barrier((values, others))[0]


def hop(array, axes, mask, size):
    return lax.ppermute(array, axes, [(j, j ^ mask) for j in range(size)])


def gather_sequence(rows):
    if (lax.axis_size("ulysses"), lax.axis_size("shard")) != (4, 4):
        return ([gather_rows(gather_rows(rows, "shard"), "ulysses")], False)
    across = hop(rows, SEQUENCE, 2, 16)
    beside = hop(rows, SEQUENCE, 1, 16)
    side = [hop(rows, SEQUENCE, 8, 16), hop(beside, SEQUENCE, 8, 16)]
    beyond = hop(after(across, side[0]), SEQUENCE, 1, 16)
    line = [rows, beside, across, beyond]
    side += [hop(across, SEQUENCE, 8, 16), hop(after(beyond, side[1]), SEQUENCE, 8, 16)]
    near = [hop(part, SEQUENCE, 4, 16) for part in line]
    far = [hop(part, SEQUENCE, 4, 16) for part in side]
    return (line + near + side + far, True)


def plane_bits():
    index = lax.axis_index(PLANE)
    return [(index >> bit) & 1 for bit in (2, 1, 0)]


def gather_line(rows):
    if lax.axis_size("shard") != 4:
        return gather_rows(rows, "shard")
    across = hop(rows, "shard", 2, 4)
    beside = hop(rows, "shard", 1, 4)
    beyond = hop(across, "shard", 1, 4)
    index = lax.axis_index("shard")
    odd, high = (index & 1) == 1, (index >> 1) == 1
    here = [jnp.where(odd, beside, rows), jnp.where(odd, rows, beside)]
    there = [jnp.where(odd, beyond, across), jnp.where(odd, across, beyond)]
    lower = [jnp.where(high, b, a) for a, b in zip(here, there)]
    upper = [jnp.where(high, a, b) for a, b in zip(here, there)]
    return jnp.concatenate(lower + upper, axis=0)


def send_far(rows):
    if lax.axis_size("batch") * lax.axis_size("ulysses") != 8:
        return [rows]
    return [rows] + [hop(rows, PLANE, mask, 8) for mask in (2, 4, 6)]


def join_near(far):
    if len(far) == 1:
        return [gather_rows(far[0], PLANE)]
    return far + [hop(part, PLANE, 1, 8) for part in far]


def send_parts(own, parts):
    for part, mask in zip(parts, RELATIVE[1:4]):
        own = own + hop(part, PLANE, mask, 8).astype(f32)
    return own


def send_line(rows):
    index = lax.axis_index("shard")
    rows = rows.reshape(2, 2, *rows.shape[1:])
    low = index & 1
    sent = hop(lax.dynamic_index_in_dim(rows, 1 - low, 1, False).astype(bf16), "shard", 1, 4)
    kept, sent = send_line_last(lax.dynamic_index_in_dim(rows, low, 1, False), sent)
    return kept + sent.astype(f32)


def send_line_last(rows, sent):
    high = lax.axis_index("shard") >> 1
    mine = [lax.dynamic_index_in_dim(part, high, 0, False) for part in (rows, sent)]
    other = [lax.dynamic_index_in_dim(part, 1 - high, 0, False) for part in (rows, sent)]
    kept = mine[0] + mine[1].astype(f32)
    return (kept, hop((other[0] + other[1].astype(f32)).astype(bf16), "shard", 2, 4))


def from_relative(blocks):
    shape = blocks.shape
    blocks = jnp.moveaxis(blocks.reshape(2, 2, 2, *shape[1:]), 0, 2)
    for axis, bit in enumerate(plane_bits()):
        blocks = jnp.where(bit == 1, jnp.flip(blocks, axis), blocks)
    return blocks.reshape(shape)


def exchange_plane(blocks):
    near = hop(blocks[4:], PLANE, 1, 8)
    own, other = [blocks[0]], [near[0]]
    for place, mask in ((1, 2), (2, 4), (3, 6)):
        pair = hop(jnp.stack([blocks[place], near[place]]), PLANE, mask, 8)
        own.append(pair[0])
        other.append(pair[1])
    return from_relative(jnp.stack(own + other))


def solution(mesh):
    nb, nu, ns = (mesh.shape[name] for name in ALL)
    devices = nb * nu * ns
    group = nu * ns
    plane = nb * nu
    repeat = group // HEADS
    cube = plane == 8 and ns == 4

    def shards(
        hidden,
        ln1_gain,
        ln1_bias,
        qkv_weight,
        qv_bias,
        out_weight,
        out_bias,
        ln2_gain,
        ln2_bias,
        fc1_weight,
        fc1_bias,
        fc2_weight,
        fc2_bias,
        cotangent,
    ):
        tok = hidden.shape[0]
        depth = qkv_weight.shape[0]
        units = fc1_weight.shape[1] // plane
        head = lax.axis_index(SEQUENCE) // repeat
        plane_index = lax.axis_index(PLANE)

        vectors = (ln1_gain, ln1_bias, qv_bias, out_bias, ln2_gain, ln2_bias, fc1_bias, fc2_bias)
        sizes = [vector.shape[0] for vector in vectors]
        extra = -(-sum(sizes) // (3 * HD))
        stride = -(-(depth + extra) // 16) * 16
        packed = 0
        for place, vector in enumerate(vectors):
            before = sum(sizes[:place])
            after_it = extra * 3 * HD - before - vector.shape[0]
            packed = packed + jnp.pad(vector, (before, after_it))
        columns = pack_columns(qkv_weight, packed.reshape(extra, 3 * HD), group, stride)
        columns = lax.all_to_all(columns, SEQUENCE, split_axis=0, concat_axis=0, tiled=True)
        pieces, mixed = gather_sequence(after(hidden, columns))
        joined = gather_rows(jnp.concatenate([out_weight, qkv_weight], axis=1), ALL)
        w_out, w_qkv = joined[:, :D], joined[:, D:]
        batch = lax.axis_index("batch")
        if nb == 2:
            lots = [columns, hop(columns, "batch", 1, 2)]
        else:
            lots = list(jnp.split(gather_rows(columns, "batch"), nb))
        packed = jnp.stack([lot.reshape(group, stride, 3 * HD)[:, depth:depth + extra] for lot in lots])
        if nb == 2:
            packed = jnp.where(batch == 0, packed, packed[::-1])
        packed = packed.reshape(devices, extra * 3 * HD)
        whole = []
        offset = 0
        for size in sizes:
            whole.append(packed[:, offset : offset + size].reshape(-1).astype(f32))
            offset += size
        gain_one, shift_one, qv_shift, out_shift, gain_two, shift_two, up_shift, down_shift = whole

        w_up = lax.all_to_all(
            after(fc1_weight, pieces[min(1, len(pieces) - 1)]), PLANE, split_axis=1, concat_axis=0, tiled=True
        )

        pieces[-1], w_up = lax.optimization_barrier((pieces[-1], w_up))

        slope = jnp.exp2(-8.0 * (head.astype(f32) + 1.0) / HEADS)
        pair = lax.dynamic_slice_in_dim(qv_shift, head * (2 * HD), 2 * HD)
        shift_head = jnp.concatenate([pair[:HD], jnp.zeros((HD,), f32), pair[HD:]])
        order = lax.axis_index(SEQUENCE) if mixed else jnp.zeros((), jnp.int32)
        normed_one, context, wide = attend_forward(
            pieces,
            lots,
            gain_one,
            shift_one,
            shift_head,
            slope,
            jnp.stack([order, batch]),
            tok,
            depth,
            stride,
        )
        context, w_up = lax.optimization_barrier((context, w_up))
        sides = [fc2_weight[:, start : start + units] for start in range(0, D, units)]
        lines = gather_rows(jnp.concatenate([w_up, *sides], axis=0), "shard")
        lines = lines.reshape(ns, -1, units)
        turned = lax.all_to_all(context, SEQUENCE, split_axis=0, concat_axis=0, tiled=True)
        turned = turned.reshape(HEADS, repeat, HD, tok)[:, 0].reshape(D, tok)
        turned, w_out = lax.optimization_barrier((turned, w_out))
        grad_plane = join_near(send_far(after(cotangent, turned)))

        inputs = hidden.astype(f32)
        attended = inputs + (dot_first(turned, w_out) + out_shift)
        normed_two, unit_two, inv_two = normalize(attended, gain_two, shift_two)
        normed_plane = join_near(send_far(normed_two.astype(bf16)))
        up_slice = lax.dynamic_slice_in_dim(up_shift, plane_index * units, units)
        place = jnp.stack([lax.axis_index("shard"), plane_index])
        if cube:
            flops = 2 * plane * tok * D * units
            activated, grad_pre, odd, grad_up_b, w_up, w_down = call_kernel(
                functools.partial(middle_kernel, tok, depth),
                "middle",
                [
                    ((plane * tok, units), bf16),
                    ((plane * tok, units), bf16),
                    ((plane // 2 * tok, D), bf16),
                    ((1, units), f32),
                    ((D, units), bf16),
                    ((units, D), bf16),
                ],
                flops * 5 // 2,
                [*normed_plane, *grad_plane, lines, up_slice.reshape(1, units)],
            )
            other = hop(odd, PLANE, 1, 8)
            own, *parts = call_kernel(
                functools.partial(pair_kernel, tok),
                "pair_sums",
                [((tok, D), f32)] + [((tok, D), bf16)] * 3,
                flops // 2,
                [grad_pre, w_up, other],
            )
            grad_norm_two = send_parts(own, parts)
            blocks = ((2, units // ns, D), (2, plane // 2 * depth, D))
            send_down, send_up, keep_down, keep_up = call_kernel(
                functools.partial(weight_kernel, tok, depth),
                "weight_grads",
                [(block, dtype) for dtype in (bf16, f32) for block in blocks],
                flops * 2,
                [*normed_plane, *grad_plane, *after((activated, grad_pre), own), place],
                1,
                [((plane * tok, D), bf16), ((plane * tok, D), bf16), ((D, units), f32)],
            )
            sent_down = hop(send_down, "shard", 1, 4)
            sent_up = hop(after(send_up, sent_down), "shard", 1, 4)
        else:
            (normed_plane,), (grad_plane,) = normed_plane, grad_plane
            w_up = lines[:, : plane * depth].reshape(ns, plane, depth, units)
            w_up = w_up.transpose(1, 0, 2, 3).reshape(D, units)
            w_down = lines[:, plane * depth :].reshape(ns, -1, units // ns, units)
            w_down = w_down.transpose(0, 2, 1, 3).reshape(units, D)
            pre_act = jnp.dot(normed_plane, w_up, preferred_element_type=f32) + up_slice
            activated, slope_act = gelu_both(pre_act)
            activated = activated.astype(bf16)
            grad_act = jnp.einsum("td,fd->tf", grad_plane, w_down, preferred_element_type=f32)
            grad_pre = (grad_act * slope_act).astype(bf16)
            grad_up_b = jnp.sum(grad_pre.astype(f32), axis=0)
            grad_norm_two = jnp.einsum("tf,df->td", grad_pre, w_up, preferred_element_type=f32)
            grad_norm_two = lax.psum_scatter(grad_norm_two, PLANE, scatter_dimension=0, tiled=True)
        grad_float = cotangent.astype(f32)
        grad_in_two, grad_gain_two, grad_shift_two = normalize_back(
            grad_norm_two, unit_two, inv_two, gain_two
        )
        grad_attended = grad_float + grad_in_two
        grad_round = grad_attended.astype(bf16)
        grad_context = dot_last(w_out, grad_round).astype(bf16).reshape(HEADS, HD, tok)
        grad_head = lax.all_to_all(
            jnp.repeat(grad_context, repeat, axis=0),
            SEQUENCE,
            split_axis=0,
            concat_axis=0,
            tiled=True,
        )
        if cube:
            late = (activated, w_down, turned, after(grad_round, grad_context), place)
            both = tok + D // plane
            (odd,) = call_kernel(
                functools.partial(late_kernel, tok, 1),
                "late_odd",
                [((plane // 2 * both, D), bf16)],
                flops // 2 + tok * D * D,
                late,
                1,
            )
            other = hop(odd, PLANE, 1, 8)
            keep_down, sent_down = send_line_last(keep_down, sent_down)
        grad_qkv_head, grad_qkv_mixed = attend_backward(
            order, wide, grad_head, tok
        )
        if cube:
            grad_qkv_head, grad_qkv_mixed, sent_up, sent_down = lax.optimization_barrier(
                (grad_qkv_head, grad_qkv_mixed, sent_up, sent_down)
            )
            own, *parts = call_kernel(
                lambda act, down, head, turned, more, index, *outs: late_kernel(
                    tok, 0, act, down, head, turned, index, more, *outs
                ),
                "late_even",
                [((both, D), f32)] + [((both, D), bf16)] * 3,
                flops // 2 + tok * D * D,
                (*late[:4], after(other, grad_qkv_head), place),
                1,
            )


        grad_qkv = lax.all_to_all(
            grad_qkv_head, SEQUENCE, split_axis=0, concat_axis=0, tiled=True
        )
        if cube:
            grad_qkv, own = lax.optimization_barrier((grad_qkv, own))
        grad_qkv = grad_qkv.reshape(HEADS, repeat, 3 * HD, tok)[:, 0].reshape(3 * D, tok)
        grad_qkv_w = jnp.einsum(
            "td,tc->dc", normed_one, grad_qkv_mixed, preferred_element_type=f32
        )
        if nb == 2:
            half = D // 2
            kept = lax.axis_index("batch")
            other = lax.dynamic_slice_in_dim(grad_qkv_w, (1 - kept) * half, half).astype(bf16)
            other = hop(other, "batch", 1, 2)
            grad_qkv_w = lax.dynamic_slice_in_dim(
                grad_qkv_w, kept * half, half
            ) + other.astype(f32)
        else:
            grad_qkv_w = lax.psum_scatter(grad_qkv_w, "batch", scatter_dimension=0, tiled=True)
        grad_norm_one = jnp.einsum("et,de->td", grad_qkv, w_qkv, preferred_element_type=f32)
        grad_qkv_w = grad_qkv_w.astype(bf16)
        if cube:
            keep_up, sent_up = send_line_last(keep_up, after(sent_up, grad_qkv))
            grad_up_w = (keep_up + sent_up.astype(f32)).astype(bf16)
            grad_up_w = grad_up_w.reshape(4, depth, 2, units).transpose(2, 0, 1, 3)
            grad_up_w = grad_up_w.reshape(plane, depth, units)
            grad_qkv_w, grad_up_w, both = lax.optimization_barrier(
                (grad_qkv_w, grad_up_w, send_parts(own, parts))
            )
            grad_up_w = exchange_plane(grad_up_w)
        unit_one, inv_one = normalize(inputs, gain_one, shift_one)[1:]
        grad_in_one, grad_gain_one, grad_shift_one = normalize_back(
            grad_norm_one, unit_one, inv_one, gain_one
        )
        input_grad = grad_attended + grad_in_one

        column_sums = jnp.sum(grad_qkv.astype(f32), axis=1).reshape(HEADS, 3, HD)
        grad_qv = jnp.stack([column_sums[:, 0], column_sums[:, 2]], axis=1).reshape(2 * D)
        grad_up_b = lax.dynamic_update_slice_in_dim(
            jnp.zeros_like(up_shift),
            grad_up_b.reshape(units),
            plane_index * units,
            0,
        )
        terms = (
            grad_gain_one,
            grad_shift_one,
            grad_qv,
            jnp.sum(grad_attended, axis=0),
            grad_gain_two,
            grad_shift_two,
            grad_up_b,
            jnp.sum(grad_float, axis=0),
        )
        terms = jnp.concatenate([term.reshape(devices, -1) for term in terms], axis=1)
        terms = lax.all_to_all(terms, ALL, split_axis=0, concat_axis=0, tiled=True)
        terms = jnp.sum(terms, axis=0)
        if cube:
            down = both[:tok]
            grad_out_w = send_line(both[tok:].reshape(ns, depth, D))
            grad_down_w = keep_down + sent_down.astype(f32)
            grad_up_w = grad_up_w.transpose(1, 0, 2).reshape(depth, plane * units).astype(f32)
        else:
            down = lax.psum_scatter(
                jnp.dot(activated, w_down, preferred_element_type=f32),
                PLANE,
                scatter_dimension=0,
                tiled=True,
            )
            grad_down_w = lax.psum_scatter(
                jnp.einsum("tf,td->fd", activated, grad_plane, preferred_element_type=f32),
                "shard",
                scatter_dimension=0,
                tiled=True,
            )
            grad_up_w = jnp.einsum(
                "td,tf->df", normed_plane, grad_pre, preferred_element_type=f32
            )
            grad_up_w = grad_up_w.reshape(plane, ns, depth, units).transpose(1, 0, 2, 3)
            grad_up_w = lax.psum_scatter(
                grad_up_w.reshape(D, units), "shard", scatter_dimension=0, tiled=True
            )
            grad_up_w = lax.all_to_all(grad_up_w, PLANE, split_axis=0, concat_axis=1, tiled=True)
            grad_out_w = jnp.einsum(
                "dt,te->de", turned, grad_round, preferred_element_type=f32
            )
            grad_out_w = lax.psum_scatter(grad_out_w, ALL, scatter_dimension=0, tiled=True)
        grad_qkv_w = lax.all_to_all(
            after(grad_qkv_w, grad_norm_one),
            SEQUENCE,
            split_axis=0,
            concat_axis=1,
            tiled=True,
        )
        grad_qkv_w = grad_qkv_w.astype(f32)
        if repeat > 1:
            grad_qkv_w = grad_qkv_w.reshape(depth, HEADS, repeat, 3 * HD)[:, :, 0].reshape(
                depth, 3 * D
            )
        output = down + down_shift + attended
        small = []
        offset = 0
        for size in sizes:
            small.append(terms[offset : offset + size])
            offset += size
        return (
            output,
            input_grad,
            small[0],
            small[1],
            grad_qkv_w,
            small[2],
            grad_out_w,
            small[3],
            small[4],
            small[5],
            grad_up_w,
            small[6],
            grad_down_w,
            small[7],
        )

    rows = P(ALL, None)
    vector = P(ALL)
    return jax.shard_map(
        shards,
        mesh=mesh,
        in_specs=(
            rows,
            vector,
            vector,
            rows,
            vector,
            rows,
            vector,
            vector,
            vector,
            rows,
            vector,
            rows,
            vector,
            rows,
        ),
        out_specs=(
            rows,
            rows,
            vector,
            vector,
            rows,
            vector,
            rows,
            vector,
            vector,
            vector,
            rows,
            vector,
            rows,
            vector,
        ),
        check_vma=False,
    )
```

```python
import functools
import math

import jax
import jax.numpy as jnp
from jax import lax
from jax.experimental import pallas as pl
from jax.experimental.pallas import tpu as pltpu
from jax.sharding import PartitionSpec as P

D = 1024
HEADS = 16
HD = 64

norm_eps = 1e-05
gelu_coef = 0.7978845608028654

ALL = ("batch", "ulysses", "shard")
SEQUENCE = ("ulysses", "shard")
PLANE = ("batch", "ulysses")
bf16 = jnp.bfloat16
f32 = jnp.float32


def normalize(inputs, gain, shift):
    center = jnp.mean(inputs, axis=-1, keepdims=True)
    centred = inputs - center
    variance = jnp.mean(centred * centred, axis=-1, keepdims=True)
    inverse = lax.rsqrt(variance + norm_eps)
    unit_rows = centred * inverse
    return (unit_rows * gain + shift, unit_rows, inverse)


def normalize_back(grad_out, unit_rows, inverse, gain):
    grad_unit = grad_out * gain
    first = jnp.mean(grad_unit, axis=-1, keepdims=True)
    second = jnp.mean(grad_unit * unit_rows, axis=-1, keepdims=True)
    grad_in = inverse * (grad_unit - first - unit_rows * second)
    return (grad_in, jnp.sum(grad_out * unit_rows, axis=0), jnp.sum(grad_out, axis=0))


def gelu_both(pre_act):
    inner = gelu_coef * (pre_act + 0.044715 * pre_act * pre_act * pre_act)
    tanh_val = jnp.tanh(inner)
    value = 0.5 * pre_act * (1.0 + tanh_val)
    slope = 0.5 * (1.0 + tanh_val) + 0.5 * pre_act * (1.0 - tanh_val * tanh_val) * gelu_coef * (
        1.0 + 3.0 * 0.044715 * pre_act * pre_act
    )
    return (value, slope)


def three_parts(column):
    high = column.astype(bf16)
    rest = column - high.astype(f32)
    middle = rest.astype(bf16)
    low = (rest - middle.astype(f32)).astype(bf16)
    return (high, middle, low)


def dot_last(left, right):
    return lax.dot_general(left, right, (((1,), (1,)), ((), ())), preferred_element_type=f32)


def pack_kernel(repeat, stride, weight_ref, vector_ref, out_ref):
    depth = weight_ref.shape[0]
    extra = vector_ref.shape[0]
    width = 3 * HD
    blank = jnp.zeros((stride - depth - extra, width), bf16)
    for place in range(out_ref.shape[0] // stride):
        head = place // repeat
        out_ref[pl.ds(place * stride, stride), :] = jnp.concatenate(
            [weight_ref[:, head * width : (head + 1) * width], vector_ref[...], blank], axis=0
        )


def pack_columns(weight, vectors, group, stride):
    return pl.pallas_call(
        functools.partial(pack_kernel, group // HEADS, stride),
        out_shape=jax.ShapeDtypeStruct((group * stride, 3 * HD), bf16),
        in_specs=[pl.BlockSpec(memory_space=pltpu.VMEM)] * 2,
        out_specs=pl.BlockSpec(memory_space=pltpu.VMEM),
        cost_estimate=pl.CostEstimate(
            flops=0, bytes_accessed=4 * weight.size, transcendentals=0
        ),
        name="pack_columns",
    )(weight, vectors)


def wide_views(wide_ref):
    return [wide_ref.at[:, 2 * HD * part : 2 * HD * (part + 1)] for part in range(4)]


def forward_kernel(block, tok, depth, stride, pieces, lots, *refs):
    piece_refs = refs[:pieces]
    lot_refs = refs[pieces : pieces + lots]
    (
        gain_ref,
        shift_ref,
        head_shift_ref,
        slope_ref,
        place_ref,
        normed_ref,
        turned_ref,
        wide_ref,
        weight_ref,
        qkv_ref,
    ) = refs[pieces + lots :]
    length = normed_ref.shape[0]
    q_ref, k_ref, v_ref, context_ref = wide_views(wide_ref)
    slope = slope_ref[0]
    for lot in range(lots):
        count = lot_refs[lot].shape[0] // stride
        if lots == 2:
            base = pl.multiple_of((place_ref[1] ^ lot) * (count * depth), count * depth)
        else:
            base = lot * count * depth
        for place in range(count):
            weight_ref[pl.ds(base + place * depth, depth), :] = lot_refs[lot][
                pl.ds(place * stride, depth), :
            ]
    gain = gain_ref[...]
    shift = shift_ref[...]
    start = 0
    for piece_ref in piece_refs:
        for first in range(0, piece_ref.shape[0], tok):
            hidden = piece_ref[pl.ds(first, tok), :].astype(f32)
            normed_ref[pl.ds(start, tok), :] = normalize(hidden, gain, shift)[0].astype(bf16)
            start += tok
    for place in range(length // tok):
        target = pl.multiple_of((place_ref[0] ^ place) * tok, tok)
        qkv_ref[pl.ds(target, tok), :] = (
            jnp.dot(
                normed_ref[pl.ds(place * tok, tok), :],
                weight_ref[...],
                preferred_element_type=f32,
            )
            + head_shift_ref[...]
        ).astype(bf16)
    for start in range(0, length, block):
        rows = pl.ds(start, block)
        qkv = qkv_ref[rows, :]
        zeros = jnp.zeros((block, HD - 6), bf16)
        ones = jnp.ones((block, 3), bf16)
        position = start + lax.broadcasted_iota(jnp.int32, (block, 1), 0)
        bias = three_parts(position.astype(f32) * slope)
        k_ref[rows, :] = jnp.concatenate([qkv[:, HD : 2 * HD], *bias, ones, zeros], axis=1)
        v_ref[rows, :] = jnp.concatenate(
            [qkv[:, 2 * HD : 3 * HD], ones, jnp.zeros((block, HD - 3), bf16)], axis=1
        )
    key_id = lax.broadcasted_iota(jnp.int32, (block, block), 1)
    row_id = lax.broadcasted_iota(jnp.int32, (block, block), 0)
    for start in range(0, length, block):
        rows = pl.ds(start, block)
        scaled = qkv_ref[rows, :HD] * bf16(1.0 / math.sqrt(HD))
        ones = jnp.ones((block, 3), bf16)
        queries = jnp.concatenate([scaled, ones, jnp.zeros((block, HD - 3), bf16)], axis=1)
        corner = jnp.where(key_id <= row_id, dot_last(queries, k_ref[rows, :]), -jnp.inf)
        top = jnp.max(corner, axis=1, keepdims=True)
        if start:
            scores = dot_last(queries, k_ref[:start, :])
            top = jnp.maximum(top, jnp.max(scores, axis=1, keepdims=True))
        accum = jnp.dot(
            jnp.exp(corner - top).astype(bf16), v_ref[rows, :], preferred_element_type=f32
        )
        if start:
            accum = accum + jnp.dot(
                jnp.exp(scores - top).astype(bf16), v_ref[:start, :], preferred_element_type=f32
            )
        total = accum[:, HD : HD + 1]
        context = (accum[:, :HD] / total).astype(bf16)
        context_ref[rows, :] = jnp.concatenate([context, jnp.zeros((block, HD), bf16)], axis=1)
        for part in range(block // tok):
            turned_ref[start // tok + part] = context[part * tok : (part + 1) * tok].T
        lse = three_parts(-(top + jnp.log(total)))
        q_ref[rows, :] = jnp.concatenate(
            [scaled, ones, *lse, jnp.zeros((block, HD - 6), bf16)], axis=1
        )


def backward_kernel(
    block,
    tok,
    order_ref,
    wide_ref,
    grad_ref,
    turned_ref,
    mixed_ref,
    gk_ref,
    gv_ref,
    out_ref,
):
    length = wide_ref.shape[0]
    q_ref, k_ref, v_ref, context_ref = wide_views(wide_ref)
    row_id = lax.broadcasted_iota(jnp.int32, (block, block), 0)
    query_id = lax.broadcasted_iota(jnp.int32, (block, block), 1)
    for start in range(0, length, block):
        rows = pl.ds(start, block)
        stop = start + block
        queries = q_ref[rows, :]
        grads = jnp.concatenate(
            [grad_ref[start // tok + part].T for part in range(block // tok)], axis=0
        )
        delta = jnp.sum(
            grads.astype(f32) * context_ref[rows, :HD].astype(f32), axis=1, keepdims=True
        )
        grads = jnp.concatenate(
            [grads, *three_parts(-delta), jnp.zeros((block, HD - 3), bf16)], axis=1
        )
        corner = jnp.where(row_id <= query_id, jnp.exp(dot_last(k_ref[rows, :], queries)), 0.0)
        corner_grad = (corner * dot_last(v_ref[rows, :], grads)).astype(bf16)
        corner = corner.astype(bf16)
        gv_ref[rows, :] = jnp.dot(corner, grads, preferred_element_type=f32)
        gk_ref[rows, :] = jnp.dot(corner_grad, queries, preferred_element_type=f32)
        grad_query = lax.dot_general(
            corner_grad, k_ref[rows, :], (((0,), (0,)), ((), ())), preferred_element_type=f32
        )
        if start:
            probs = jnp.exp(dot_last(k_ref[:start, :], queries))
            probs_grad = (probs * dot_last(v_ref[:start, :], grads)).astype(bf16)
            probs = probs.astype(bf16)
            gv_ref[:start, :] += jnp.dot(probs, grads, preferred_element_type=f32)
            gk_ref[:start, :] += jnp.dot(probs_grad, queries, preferred_element_type=f32)
            grad_query = grad_query + lax.dot_general(
                probs_grad, k_ref[:start, :], (((0,), (0,)), ((), ())), preferred_element_type=f32
            )
        out_ref[rows, :HD] = (grad_query[:, :HD] * (1.0 / math.sqrt(HD))).astype(bf16)
    for start in range(0, length, block):
        rows = pl.ds(start, block)
        out_ref[rows, HD : 2 * HD] = gk_ref[rows, :HD].astype(bf16)
        out_ref[rows, 2 * HD : 3 * HD] = gv_ref[rows, :HD].astype(bf16)
    for place in range(length // tok):
        target = pl.multiple_of((order_ref[0] ^ place) * tok, tok)
        part = out_ref[pl.ds(place * tok, tok), :]
        mixed_ref[pl.ds(target, tok), :] = part
        turned_ref[place] = part.T


def block_of(length):
    return max(256, length // 8) if length % 256 == 0 else length


def attend_forward(pieces, lots, gain, shift, head_shift, slope, place, tok, depth, stride):
    length = sum(piece.shape[0] for piece in pieces)
    vmem = pl.BlockSpec(memory_space=pltpu.VMEM)
    smem = pl.BlockSpec(memory_space=pltpu.SMEM)
    return pl.pallas_call(
        functools.partial(
            forward_kernel, block_of(length), tok, depth, stride, len(pieces), len(lots)
        ),
        out_shape=(
            jax.ShapeDtypeStruct((length, D), bf16),
            jax.ShapeDtypeStruct((length // tok, HD, tok), bf16),
            jax.ShapeDtypeStruct((length, 8 * HD), bf16),
        ),
        in_specs=[vmem] * (len(pieces) + len(lots) + 3) + [smem, smem],
        out_specs=(vmem,) * 3,
        scratch_shapes=[pltpu.VMEM((D, 3 * HD), bf16), pltpu.VMEM((length, 3 * HD), bf16)],
        compiler_params=pltpu.CompilerParams(vmem_limit_bytes=56 * 2**20),
        cost_estimate=pl.CostEstimate(
            flops=length * length * 512 + length * D * 400,
            bytes_accessed=length * D * 4,
            transcendentals=length * length // 2,
        ),
        name="attend_forward",
    )(
        *pieces,
        *lots,
        gain.reshape(1, -1),
        shift.reshape(1, -1),
        head_shift.reshape(1, -1),
        slope.reshape(1),
        place,
    )


def attend_backward(order, wide, grad_context, tok):
    length = wide.shape[0]
    vmem = pl.BlockSpec(memory_space=pltpu.VMEM)
    return pl.pallas_call(
        functools.partial(backward_kernel, block_of(length), tok),
        out_shape=(
            jax.ShapeDtypeStruct((length // tok, 3 * HD, tok), bf16),
            jax.ShapeDtypeStruct((length, 3 * HD), bf16),
        ),
        in_specs=[pl.BlockSpec(memory_space=pltpu.SMEM)] + [vmem] * 2,
        out_specs=(vmem, vmem),
        scratch_shapes=[
            pltpu.VMEM((length, 2 * HD), f32),
            pltpu.VMEM((length, 2 * HD), f32),
            pltpu.VMEM((length, 3 * HD), bf16),
        ],
        compiler_params=pltpu.CompilerParams(vmem_limit_bytes=48 * 2**20),
        cost_estimate=pl.CostEstimate(
            flops=length * length * 1280,
            bytes_accessed=length * 2048,
            transcendentals=length * length // 2,
        ),
        name="attend_backward",
    )(order.reshape(1), wide, grad_context)


RELATIVE = (0, 2, 4, 6, 1, 3, 5, 7)


def dot_first(left, right):
    return lax.dot_general(left, right, (((0,), (0,)), ((), ())), preferred_element_type=f32)


def middle_kernel(tok, depth, *refs):
    normed_refs, grad_refs = refs[:8], refs[8:16]
    lines_ref, shift_ref, act_ref, pre_ref, odd_ref, sum_ref, up_ref, down_ref = refs[16:]
    sums = jnp.zeros(sum_ref.shape, f32)
    units = up_ref.shape[1]
    part = units // 4
    for line in range(4):
        for place in range(8):
            up_ref[pl.ds((place * 4 + line) * depth, depth), :] = lines_ref[
                line, pl.ds(place * depth, depth), :
            ]
        for side in range(D // units):
            down_ref[pl.ds(line * part, part), side * units : (side + 1) * units] = lines_ref[
                line, pl.ds(8 * depth + side * part, part), :
            ]
    for pair in (2, 3, 0, 1):
        rows = pl.ds(2 * pair * tok, 2 * tok)
        normed = jnp.concatenate([ref[...] for ref in normed_refs[2 * pair : 2 * pair + 2]], axis=0)
        grads = jnp.concatenate([ref[...] for ref in grad_refs[2 * pair : 2 * pair + 2]], axis=0)
        pre_act = jnp.dot(normed, up_ref[...], preferred_element_type=f32) + shift_ref[...]
        value, slope = gelu_both(pre_act)
        grad_pre = (dot_last(grads, down_ref[...]) * slope).astype(bf16)
        act_ref[rows, :] = value.astype(bf16)
        pre_ref[rows, :] = grad_pre
        sums = sums + jnp.sum(grad_pre.astype(f32), axis=0, keepdims=True)
        if pair >= 2:
            odd_ref[pl.ds(2 * (pair - 2) * tok, 2 * tok), :] = dot_last(
                grad_pre, up_ref[...]
            ).astype(bf16)
    sum_ref[...] = sums


def weight_kernel(tok, depth, *refs):
    normed_refs, grad_refs = refs[:8], refs[8:16]
    act_ref, pre_ref, place_ref, *out_refs = refs[16:23]
    normed_ref, grad_ref, up_ref = refs[23:]
    units = pre_ref.shape[1]
    part = units // 4
    for place in range(8):
        normed_ref[pl.ds(place * tok, tok), :] = normed_refs[place][...]
        grad_ref[pl.ds(place * tok, tok), :] = grad_refs[place][...]
    for start in range(0, D, 256):
        up_ref[pl.ds(start, 256), :] = dot_first(normed_ref[:, start : start + 256], pre_ref[...])
    low = place_ref[0] & 1
    for high in range(2):
        for (first_ref, second_ref), bit in ((out_refs[:2], 1 - low), (out_refs[2:], low)):
            line = 2 * high + bit
            columns = pl.ds(pl.multiple_of(line * part, part), part)
            first_ref[high] = dot_first(act_ref[:, columns], grad_ref[...]).astype(first_ref.dtype)
            for place, mask in enumerate(RELATIVE):
                source = ((place_ref[1] ^ mask) * 4 + line) * depth
                second_ref[
                    high,
                    place % 4 * depth : (place % 4 + 1) * depth,
                    place // 4 * units : (place // 4 + 1) * units,
                ] = up_ref[pl.ds(pl.multiple_of(source, depth), depth), :].astype(second_ref.dtype)


def pair_kernel(tok, pre_ref, up_ref, other_ref, own_ref, *part_refs):
    for place in range(4):
        rows = pl.ds(place * tok, tok)
        pair = dot_last(pre_ref[rows, :], up_ref[...]) + other_ref[rows, :].astype(f32)
        out_ref = part_refs[place - 1] if place else own_ref
        out_ref[...] = pair.astype(out_ref.dtype)


def late_kernel(tok, odd, act_ref, down_ref, context_ref, round_ref, place_ref, *refs):
    width = context_ref.shape[0] // 8
    for place in range(4):
        act = act_ref[pl.ds((4 * odd + place) * tok, tok), :]
        rows = jnp.dot(act, down_ref[...], preferred_element_type=f32)
        block = place_ref[1] ^ RELATIVE[4 * odd + place]
        columns = pl.ds(pl.multiple_of(block * width, width), width)
        weight = jnp.dot(context_ref[columns, :], round_ref[...], preferred_element_type=f32)
        first = pl.ds(place * (tok + width), tok)
        second = pl.ds(place * (tok + width) + tok, width)
        if odd:
            refs[0][first, :] = rows.astype(bf16)
            refs[0][second, :] = weight.astype(bf16)
        else:
            out_ref = refs[1 + place]
            out_ref[:tok, :] = (rows + refs[0][first, :].astype(f32)).astype(out_ref.dtype)
            out_ref[tok:, :] = (weight + refs[0][second, :].astype(f32)).astype(out_ref.dtype)


def call_kernel(kernel, name, outs, flops, values, scalars=0, scratch=()):
    vmem = pl.BlockSpec(memory_space=pltpu.VMEM)
    smem = pl.BlockSpec(memory_space=pltpu.SMEM)
    outs = [jax.ShapeDtypeStruct(shape, dtype) for shape, dtype in outs]
    size = sum(value.size * value.dtype.itemsize for value in (*values, *outs))
    return pl.pallas_call(
        kernel,
        out_shape=outs,
        in_specs=[vmem] * (len(values) - scalars) + [smem] * scalars,
        out_specs=[vmem] * len(outs),
        scratch_shapes=[pltpu.VMEM(shape, dtype) for shape, dtype in scratch],
        compiler_params=pltpu.CompilerParams(vmem_limit_bytes=48 * 2**20),
        cost_estimate=pl.CostEstimate(flops=flops, bytes_accessed=size, transcendentals=0),
        name=name,
    )(*values)


def gather_rows(rows, axis):
    return lax.all_gather(rows, axis, axis=0, tiled=True)


def after(values, *others):
    return lax.optimization_barrier((values, others))[0]


def hop(array, axes, mask, size):
    return lax.ppermute(array, axes, [(j, j ^ mask) for j in range(size)])


def gather_sequence(rows):
    if (lax.axis_size("ulysses"), lax.axis_size("shard")) != (4, 4):
        return ([gather_rows(gather_rows(rows, "shard"), "ulysses")], False)
    across = hop(rows, SEQUENCE, 2, 16)
    beside = hop(rows, SEQUENCE, 1, 16)
    side = [hop(rows, SEQUENCE, 8, 16), hop(beside, SEQUENCE, 8, 16)]
    beyond = hop(after(across, side), SEQUENCE, 1, 16)
    line = [rows, beside, across, beyond]
    side += [hop(across, SEQUENCE, 8, 16)]
    side += [hop(after(beyond, side[2]), SEQUENCE, 8, 16)]
    near = [hop(part, SEQUENCE, 4, 16) for part in line]
    far = [hop(part, SEQUENCE, 4, 16) for part in side]
    return (line + near + side + far, True)


def plane_bits():
    index = lax.axis_index(PLANE)
    return [(index >> bit) & 1 for bit in (2, 1, 0)]


def gather_line(rows):
    if lax.axis_size("shard") != 4:
        return gather_rows(rows, "shard")
    across = hop(rows, "shard", 2, 4)
    beside = hop(rows, "shard", 1, 4)
    beyond = hop(across, "shard", 1, 4)
    index = lax.axis_index("shard")
    odd, high = (index & 1) == 1, (index >> 1) == 1
    here = [jnp.where(odd, beside, rows), jnp.where(odd, rows, beside)]
    there = [jnp.where(odd, beyond, across), jnp.where(odd, across, beyond)]
    lower = [jnp.where(high, b, a) for a, b in zip(here, there)]
    upper = [jnp.where(high, a, b) for a, b in zip(here, there)]
    return jnp.concatenate(lower + upper, axis=0)


def send_far(rows):
    if lax.axis_size("batch") * lax.axis_size("ulysses") != 8:
        return [rows]
    return [rows] + [hop(rows, PLANE, mask, 8) for mask in (2, 4, 6)]


def join_near(far):
    if len(far) == 1:
        return [gather_rows(far[0], PLANE)]
    return far + [hop(part, PLANE, 1, 8) for part in far]


def send_parts(own, parts):
    for part, mask in zip(parts, RELATIVE[1:4]):
        own = own + hop(part, PLANE, mask, 8).astype(f32)
    return own


def send_line(rows):
    index = lax.axis_index("shard")
    rows = rows.reshape(2, 2, *rows.shape[1:])
    low = index & 1
    sent = hop(lax.dynamic_index_in_dim(rows, 1 - low, 1, False).astype(bf16), "shard", 1, 4)
    kept, sent = send_line_last(lax.dynamic_index_in_dim(rows, low, 1, False), sent)
    return kept + sent.astype(f32)


def send_line_last(rows, sent):
    high = lax.axis_index("shard") >> 1
    mine = [lax.dynamic_index_in_dim(part, high, 0, False) for part in (rows, sent)]
    other = [lax.dynamic_index_in_dim(part, 1 - high, 0, False) for part in (rows, sent)]
    kept = mine[0] + mine[1].astype(f32)
    return (kept, hop((other[0] + other[1].astype(f32)).astype(bf16), "shard", 2, 4))


def from_relative(blocks):
    shape = blocks.shape
    blocks = jnp.moveaxis(blocks.reshape(2, 2, 2, *shape[1:]), 0, 2)
    for axis, bit in enumerate(plane_bits()):
        blocks = jnp.where(bit == 1, jnp.flip(blocks, axis), blocks)
    return blocks.reshape(shape)


def exchange_plane(blocks):
    near = hop(blocks[4:], PLANE, 1, 8)
    own, other = [blocks[0]], [near[0]]
    for place, mask in ((1, 2), (2, 4), (3, 6)):
        pair = hop(jnp.stack([blocks[place], near[place]]), PLANE, mask, 8)
        own.append(pair[0])
        other.append(pair[1])
    return from_relative(jnp.stack(own + other))


def solution(mesh):
    nb, nu, ns = (mesh.shape[name] for name in ALL)
    devices = nb * nu * ns
    group = nu * ns
    plane = nb * nu
    repeat = group // HEADS
    cube = plane == 8 and ns == 4

    def shards(
        hidden,
        ln1_gain,
        ln1_bias,
        qkv_weight,
        qv_bias,
        out_weight,
        out_bias,
        ln2_gain,
        ln2_bias,
        fc1_weight,
        fc1_bias,
        fc2_weight,
        fc2_bias,
        cotangent,
    ):
        tok = hidden.shape[0]
        depth = qkv_weight.shape[0]
        units = fc1_weight.shape[1] // plane
        head = lax.axis_index(SEQUENCE) // repeat
        plane_index = lax.axis_index(PLANE)

        vectors = (ln1_gain, ln1_bias, qv_bias, out_bias, ln2_gain, ln2_bias, fc1_bias, fc2_bias)
        sizes = [vector.shape[0] for vector in vectors]
        extra = -(-sum(sizes) // (3 * HD))
        stride = -(-(depth + extra) // 16) * 16
        packed = 0
        for place, vector in enumerate(vectors):
            before = sum(sizes[:place])
            after_it = extra * 3 * HD - before - vector.shape[0]
            packed = packed + jnp.pad(vector, (before, after_it))
        columns = pack_columns(qkv_weight, packed.reshape(extra, 3 * HD), group, stride)
        columns = lax.all_to_all(columns, SEQUENCE, split_axis=0, concat_axis=0, tiled=True)
        pieces, mixed = gather_sequence(after(hidden, columns))
        joined = gather_rows(jnp.concatenate([out_weight, qkv_weight], axis=1), ALL)
        w_out, w_qkv = joined[:, :D], joined[:, D:]
        batch = lax.axis_index("batch")
        if nb == 2:
            lots = [columns, hop(columns, "batch", 1, 2)]
        else:
            lots = list(jnp.split(gather_rows(columns, "batch"), nb))
        packed = jnp.stack([lot.reshape(group, stride, 3 * HD)[:, depth:depth + extra] for lot in lots])
        if nb == 2:
            packed = jnp.where(batch == 0, packed, packed[::-1])
        packed = packed.reshape(devices, extra * 3 * HD)
        whole = []
        offset = 0
        for size in sizes:
            whole.append(packed[:, offset : offset + size].reshape(-1).astype(f32))
            offset += size
        gain_one, shift_one, qv_shift, out_shift, gain_two, shift_two, up_shift, down_shift = whole

        w_up = lax.all_to_all(
            after(fc1_weight, pieces[min(1, len(pieces) - 1)]), PLANE, split_axis=1, concat_axis=0, tiled=True
        )

        pieces[-1], w_up = lax.optimization_barrier((pieces[-1], w_up))

        slope = jnp.exp2(-8.0 * (head.astype(f32) + 1.0) / HEADS)
        pair = lax.dynamic_slice_in_dim(qv_shift, head * (2 * HD), 2 * HD)
        shift_head = jnp.concatenate([pair[:HD], jnp.zeros((HD,), f32), pair[HD:]])
        order = lax.axis_index(SEQUENCE) if mixed else jnp.zeros((), jnp.int32)
        normed_one, context, wide = attend_forward(
            pieces,
            lots,
            gain_one,
            shift_one,
            shift_head,
            slope,
            jnp.stack([order, batch]),
            tok,
            depth,
            stride,
        )
        context, w_up = lax.optimization_barrier((context, w_up))
        sides = [fc2_weight[:, start : start + units] for start in range(0, D, units)]
        lines = gather_rows(jnp.concatenate([w_up, *sides], axis=0), "shard")
        lines = lines.reshape(ns, -1, units)
        turned = lax.all_to_all(context, SEQUENCE, split_axis=0, concat_axis=0, tiled=True)
        turned = turned.reshape(HEADS, repeat, HD, tok)[:, 0].reshape(D, tok)
        turned, w_out = lax.optimization_barrier((turned, w_out))
        grad_plane = join_near(send_far(after(cotangent, turned)))

        inputs = hidden.astype(f32)
        attended = inputs + (dot_first(turned, w_out) + out_shift)
        normed_two, unit_two, inv_two = normalize(attended, gain_two, shift_two)
        normed_plane = join_near(send_far(normed_two.astype(bf16)))
        up_slice = lax.dynamic_slice_in_dim(up_shift, plane_index * units, units)
        place = jnp.stack([lax.axis_index("shard"), plane_index])
        if cube:
            flops = 2 * plane * tok * D * units
            activated, grad_pre, odd, grad_up_b, w_up, w_down = call_kernel(
                functools.partial(middle_kernel, tok, depth),
                "middle",
                [
                    ((plane * tok, units), bf16),
                    ((plane * tok, units), bf16),
                    ((plane // 2 * tok, D), bf16),
                    ((1, units), f32),
                    ((D, units), bf16),
                    ((units, D), bf16),
                ],
                flops * 5 // 2,
                [*normed_plane, *grad_plane, lines, up_slice.reshape(1, units)],
            )
            other = hop(odd, PLANE, 1, 8)
            own, *parts = call_kernel(
                functools.partial(pair_kernel, tok),
                "pair_sums",
                [((tok, D), f32)] + [((tok, D), bf16)] * 3,
                flops // 2,
                [grad_pre, w_up, other],
            )
            grad_norm_two = send_parts(own, parts)
            blocks = ((2, units // ns, D), (2, plane // 2 * depth, D))
            send_down, send_up, keep_down, keep_up = call_kernel(
                functools.partial(weight_kernel, tok, depth),
                "weight_grads",
                [(block, dtype) for dtype in (bf16, f32) for block in blocks],
                flops * 2,
                [*normed_plane, *grad_plane, *after((activated, grad_pre), own), place],
                1,
                [((plane * tok, D), bf16), ((plane * tok, D), bf16), ((D, units), f32)],
            )
            sent_down = hop(send_down, "shard", 1, 4)
            sent_up = hop(after(send_up, sent_down), "shard", 1, 4)
        else:
            (normed_plane,), (grad_plane,) = normed_plane, grad_plane
            w_up = lines[:, : plane * depth].reshape(ns, plane, depth, units)
            w_up = w_up.transpose(1, 0, 2, 3).reshape(D, units)
            w_down = lines[:, plane * depth :].reshape(ns, -1, units // ns, units)
            w_down = w_down.transpose(0, 2, 1, 3).reshape(units, D)
            pre_act = jnp.dot(normed_plane, w_up, preferred_element_type=f32) + up_slice
            activated, slope_act = gelu_both(pre_act)
            activated = activated.astype(bf16)
            grad_act = jnp.einsum("td,fd->tf", grad_plane, w_down, preferred_element_type=f32)
            grad_pre = (grad_act * slope_act).astype(bf16)
            grad_up_b = jnp.sum(grad_pre.astype(f32), axis=0)
            grad_norm_two = jnp.einsum("tf,df->td", grad_pre, w_up, preferred_element_type=f32)
            grad_norm_two = lax.psum_scatter(grad_norm_two, PLANE, scatter_dimension=0, tiled=True)
        grad_float = cotangent.astype(f32)
        grad_in_two, grad_gain_two, grad_shift_two = normalize_back(
            grad_norm_two, unit_two, inv_two, gain_two
        )
        grad_attended = grad_float + grad_in_two
        grad_round = grad_attended.astype(bf16)
        grad_context = dot_last(w_out, grad_round).astype(bf16).reshape(HEADS, HD, tok)
        grad_head = lax.all_to_all(
            jnp.repeat(grad_context, repeat, axis=0),
            SEQUENCE,
            split_axis=0,
            concat_axis=0,
            tiled=True,
        )
        if cube:
            late = (activated, w_down, turned, after(grad_round, grad_context), place)
            both = tok + D // plane
            (odd,) = call_kernel(
                functools.partial(late_kernel, tok, 1),
                "late_odd",
                [((plane // 2 * both, D), bf16)],
                flops // 2 + tok * D * D,
                late,
                1,
            )
            other = hop(odd, PLANE, 1, 8)
            keep_down, sent_down = send_line_last(keep_down, sent_down)
        grad_qkv_head, grad_qkv_mixed = attend_backward(
            order, wide, grad_head, tok
        )
        if cube:
            grad_qkv_head, grad_qkv_mixed, sent_up, sent_down = lax.optimization_barrier(
                (grad_qkv_head, grad_qkv_mixed, sent_up, sent_down)
            )
            own, *parts = call_kernel(
                lambda act, down, head, turned, more, index, *outs: late_kernel(
                    tok, 0, act, down, head, turned, index, more, *outs
                ),
                "late_even",
                [((both, D), f32)] + [((both, D), bf16)] * 3,
                flops // 2 + tok * D * D,
                (*late[:4], after(other, grad_qkv_head), place),
                1,
            )


        grad_qkv = lax.all_to_all(
            grad_qkv_head, SEQUENCE, split_axis=0, concat_axis=0, tiled=True
        )
        if cube:
            grad_qkv, own = lax.optimization_barrier((grad_qkv, own))
        grad_qkv = grad_qkv.reshape(HEADS, repeat, 3 * HD, tok)[:, 0].reshape(3 * D, tok)
        grad_qkv_w = jnp.einsum(
            "td,tc->dc", normed_one, grad_qkv_mixed, preferred_element_type=f32
        )
        if nb == 2:
            half = D // 2
            kept = lax.axis_index("batch")
            other = lax.dynamic_slice_in_dim(grad_qkv_w, (1 - kept) * half, half).astype(bf16)
            other = hop(other, "batch", 1, 2)
            grad_qkv_w = lax.dynamic_slice_in_dim(
                grad_qkv_w, kept * half, half
            ) + other.astype(f32)
        else:
            grad_qkv_w = lax.psum_scatter(grad_qkv_w, "batch", scatter_dimension=0, tiled=True)
        grad_norm_one = jnp.einsum("et,de->td", grad_qkv, w_qkv, preferred_element_type=f32)
        grad_qkv_w = grad_qkv_w.astype(bf16)
        if cube:
            keep_up, sent_up = send_line_last(keep_up, after(sent_up, grad_qkv))
            grad_up_w = (keep_up + sent_up.astype(f32)).astype(bf16)
            grad_up_w = grad_up_w.reshape(4, depth, 2, units).transpose(2, 0, 1, 3)
            grad_up_w = grad_up_w.reshape(plane, depth, units)
            grad_qkv_w, grad_up_w, both = lax.optimization_barrier(
                (grad_qkv_w, grad_up_w, send_parts(own, parts))
            )
            grad_up_w = exchange_plane(grad_up_w)
        unit_one, inv_one = normalize(inputs, gain_one, shift_one)[1:]
        grad_in_one, grad_gain_one, grad_shift_one = normalize_back(
            grad_norm_one, unit_one, inv_one, gain_one
        )
        input_grad = grad_attended + grad_in_one

        column_sums = jnp.sum(grad_qkv.astype(f32), axis=1).reshape(HEADS, 3, HD)
        grad_qv = jnp.stack([column_sums[:, 0], column_sums[:, 2]], axis=1).reshape(2 * D)
        grad_up_b = lax.dynamic_update_slice_in_dim(
            jnp.zeros_like(up_shift),
            grad_up_b.reshape(units),
            plane_index * units,
            0,
        )
        terms = (
            grad_gain_one,
            grad_shift_one,
            grad_qv,
            jnp.sum(grad_attended, axis=0),
            grad_gain_two,
            grad_shift_two,
            grad_up_b,
            jnp.sum(grad_float, axis=0),
        )
        terms = jnp.concatenate([term.reshape(devices, -1) for term in terms], axis=1)
        terms = lax.all_to_all(terms, ALL, split_axis=0, concat_axis=0, tiled=True)
        terms = jnp.sum(terms, axis=0)
        if cube:
            down = both[:tok]
            grad_out_w = send_line(both[tok:].reshape(ns, depth, D))
            grad_down_w = keep_down + sent_down.astype(f32)
            grad_up_w = grad_up_w.transpose(1, 0, 2).reshape(depth, plane * units).astype(f32)
        else:
            down = lax.psum_scatter(
                jnp.dot(activated, w_down, preferred_element_type=f32),
                PLANE,
                scatter_dimension=0,
                tiled=True,
            )
            grad_down_w = lax.psum_scatter(
                jnp.einsum("tf,td->fd", activated, grad_plane, preferred_element_type=f32),
                "shard",
                scatter_dimension=0,
                tiled=True,
            )
            grad_up_w = jnp.einsum(
                "td,tf->df", normed_plane, grad_pre, preferred_element_type=f32
            )
            grad_up_w = grad_up_w.reshape(plane, ns, depth, units).transpose(1, 0, 2, 3)
            grad_up_w = lax.psum_scatter(
                grad_up_w.reshape(D, units), "shard", scatter_dimension=0, tiled=True
            )
            grad_up_w = lax.all_to_all(grad_up_w, PLANE, split_axis=0, concat_axis=1, tiled=True)
            grad_out_w = jnp.einsum(
                "dt,te->de", turned, grad_round, preferred_element_type=f32
            )
            grad_out_w = lax.psum_scatter(grad_out_w, ALL, scatter_dimension=0, tiled=True)
        grad_qkv_w = lax.all_to_all(
            after(grad_qkv_w, grad_norm_one),
            SEQUENCE,
            split_axis=0,
            concat_axis=1,
            tiled=True,
        )
        grad_qkv_w = grad_qkv_w.astype(f32)
        if repeat > 1:
            grad_qkv_w = grad_qkv_w.reshape(depth, HEADS, repeat, 3 * HD)[:, :, 0].reshape(
                depth, 3 * D
            )
        output = down + down_shift + attended
        small = []
        offset = 0
        for size in sizes:
            small.append(terms[offset : offset + size])
            offset += size
        return (
            output,
            input_grad,
            small[0],
            small[1],
            grad_qkv_w,
            small[2],
            grad_out_w,
            small[3],
            small[4],
            small[5],
            grad_up_w,
            small[6],
            grad_down_w,
            small[7],
        )

    rows = P(ALL, None)
    vector = P(ALL)
    return jax.shard_map(
        shards,
        mesh=mesh,
        in_specs=(
            rows,
            vector,
            vector,
            rows,
            vector,
            rows,
            vector,
            vector,
            vector,
            rows,
            vector,
            rows,
            vector,
            rows,
        ),
        out_specs=(
            rows,
            rows,
            vector,
            vector,
            rows,
            vector,
            rows,
            vector,
            vector,
            vector,
            rows,
            vector,
            rows,
            vector,
        ),
        check_vma=False,
    )
```
